128 devices in a mesh: dp: 16 (over x, y), tensor: 8 (over z, core).
Axes of the slice: x: 4, y: 4, z: 4, core: 2. Of those that a mesh axis runs over, the one named last changes fastest.
Arguments:
- out_grad: bfloat16 [16384, 5120], P(('dp', 'tensor')), may hold values from -0.796875 to 0.796875
- normed: bfloat16 [16384, 5120], P(('dp', 'tensor')), may hold values from -24 to 24
- router: bfloat16 [5120, 128], replicated, may hold values from -1 to 1
- expert_ids: int32 [16384, 6], P(('dp', 'tensor')), may hold values from 0 to 127, all different within a row; in each aligned block of 128 rows (0 to 127, 128 to 255, ...) at most 8 rows name the same one
- hidden_act: bfloat16 [128, 1024, 768], P(('dp', 'tensor')), may hold values from -6 to 6
- down_weight: bfloat16 [128, 768, 5120], P(('dp', 'tensor')), may hold values from -0.21875 to 0.21875
Outputs:
- d_down: bfloat16 [128, 768, 5120], P(('dp', 'tensor'))
- d_hidden: bfloat16 [128, 1024, 768], P(('dp', 'tensor'))
- d_router: float32 [5120, 128], P(('dp', 'tensor'))
- d_normed: bfloat16 [16384, 5120], P(('dp', 'tensor'))
The draws below stay inside these ranges and needn't reach their ends.
Inputs may be any that keep to these rules, and one draw needn't show every extreme that they name: `expert_ids`: each row names 6 different experts; within the 128 rows of one device no expert is named more than 8 times, and in every draw some expert is named exactly 8 times by the rows of some device.
All inputs are finite; a program needn't handle non-finite values.
Results may differ from the reference program's by a relative error of at most 0.034.
Values may be sent and summed in bfloat16 or wider, within the bound.
No kernel may reach another device: no remote copies, remote signals or barrier semaphores. Data moves between devices by JAX's collectives and lax.ppermute only.
A program may use at most 128 MiB of HBM per device.

```python
import math
import jax
import jax.numpy as jnp
import numpy as np
from jax import lax

D = 5120
H = 768
TOP = 6
TOK_DEV = 128
EXPERTS = 128
TOKENS = 16384
CAP = 8
N_DP = 16
N_TENSOR = 8


def draw_router(key, part):
    key = jax.random.fold_in(key, 3)
    values = jax.random.normal(key, (D, EXPERTS), jnp.float32) * (1.0 / math.sqrt(D))
    return jnp.clip(values, -1.0, 1.0).astype(jnp.bfloat16)


def draw_normed(key, part):
    key = jax.random.fold_in(key, 4)
    values = jax.random.normal(key, (TOKENS, D), jnp.float32)
    blocks = TOKENS // TOK_DEV
    span = D // blocks
    pairing = jax.random.permutation(jax.random.fold_in(key, 5), blocks)
    row_block = jnp.arange(TOKENS) // TOK_DEV
    col_block = jnp.arange(D) // span
    values = values * jnp.where(pairing[row_block][:, None] == col_block[None, :], 4.0, 1.0)
    return jnp.clip(values, -24.0, 24.0).astype(jnp.bfloat16)


def steps_of(rng, shape, cuts, least, top_value):
    loudness = 1.0
    for axis_at, blocks in cuts:
        steps = jax.random.uniform(jax.random.fold_in(jax.random.fold_in(rng, 6), axis_at), (blocks,), jnp.float32, least / len(cuts), top_value / len(cuts))
        loudness = loudness * jnp.repeat(jnp.exp(steps), shape[axis_at] // blocks).reshape((-1,) + (1,) * (len(shape) - 1 - axis_at))
    return loudness


def routed_block(rng, own, number, rows, amount, top, reach, skew):
    ranking = jax.random.permutation(rng, amount)
    packed, ordinary = shares(amount, rows * top, reach, skew, True), shares(amount, rows * top, reach, skew, False)
    places = jnp.arange(amount)

    def named(sizes, offset_by):
        used = int((sizes > 0).sum())
        fixed = max(1, used // 4)
        passed = fixed + (places - fixed + offset_by * (used - fixed)) % max(1, amount - fixed)
        return jnp.zeros((amount,), jnp.int32).at[ranking[jnp.where(places < fixed, places, passed)]].set(jnp.asarray(sizes, jnp.int32))

    sizes = jnp.where(number % 4 == 0, named(packed, number // 4), named(ordinary, number - number // 4 - 1))
    mixed = jax.random.permutation(jax.random.fold_in(own, 3), amount)
    giver, sink = mixed[0:amount // 2 * 2:2], mixed[1:amount // 2 * 2:2]
    slack = jnp.minimum(sizes[giver] - 1, reach - sizes[sink]) // 2
    slack = jnp.where((giver == ranking[0]) | (sink == ranking[0]) | (sizes[sink] == 0), 0, jnp.maximum(slack, 0))
    passed = jax.random.randint(jax.random.fold_in(own, 4), (amount // 2,), 0, 1 << 20) % (slack + 1)
    sizes = sizes.at[giver].add(-passed).at[sink].add(passed)
    items = jnp.searchsorted(jnp.cumsum(sizes), jnp.arange(rows * top), side="right").astype(jnp.int32)
    table = items.reshape(top, rows).T
    table = table[jax.random.permutation(jax.random.fold_in(own, 1), rows)]
    offset_by = jax.random.randint(jax.random.fold_in(own, 2), (rows, 1), 0, top)
    return jnp.take_along_axis(table, (jnp.arange(top)[None, :] + offset_by) % top, axis=1)


def shares(count, total, reach, lean, full):
    portions = [(1 << 20) // math.isqrt(grade ** lean) + 1 for grade in range(1, count + 1)]
    largest = reach if full else min(reach, max(-(-total // count), total * portions[0] // sum(portions)))
    least = 1 if total - largest >= count - 1 else 0
    holding, rest = [largest] + [least] * (count - 1), total - largest - least * (count - 1)
    while rest > 0:
        free = [i for i in range(1, count) if holding[i] < largest] or [i for i in range(1, count) if holding[i] < reach]
        pool, remaining = sum([portions[i] for i in free]), rest
        for i in free:
            more = min(reach - holding[i], max(1, remaining * portions[i] // pool), rest)
            holding[i] = holding[i] + more
            rest = rest - more
    return np.array(holding)


def centred(own_key, extent, spread, bound, split=(), kind=jnp.bfloat16):
    drawn = spread * jax.random.normal(own_key, extent, jnp.float32)
    if split:
        drawn = drawn * steps_of(own_key, extent, split, -0.22, 0.18)
    return jnp.clip(drawn, -bound, bound).astype(kind)


def setup_inputs(seed: int = 0) -> dict:
    splits = jax.random.split(jax.random.key(seed), 7)
    out_grad = centred(splits[0], (TOKENS, D), 0.1, 0.796875, ((0, 128),))
    normed = draw_normed(jax.random.fold_in(splits[6], 71), 0)
    router = draw_router(jax.random.fold_in(splits[6], 71), 0)
    expert_ids_keys = jax.random.split(jax.random.fold_in(splits[3], 1), TOKENS // TOK_DEV)
    expert_ids_turns = jax.random.permutation(jax.random.fold_in(splits[3], 3), TOKENS // TOK_DEV)
    expert_ids = jax.vmap(lambda own, number: routed_block(jax.random.fold_in(splits[3], 2), own, number, TOK_DEV, EXPERTS, TOP, CAP, 2))(expert_ids_keys, expert_ids_turns).reshape((TOKENS, TOP))
    hidden_act = centred(splits[4], (EXPERTS, N_DP * N_TENSOR * CAP, H), 1.0, 6.0, ((0, 128),))
    down_weight = centred(splits[5], (EXPERTS, H, D), H ** -0.5, 0.21875, ((0, 128),))
    return {"out_grad": out_grad, "normed": normed, "router": router, "expert_ids": expert_ids, "hidden_act": hidden_act, "down_weight": down_weight}


route_scale = 16.0


def slot_ranks(expert_ids):
    groups = N_DP * N_TENSOR
    flat_ids = expert_ids.reshape(groups, TOK_DEV * TOP)
    expert_range = jnp.arange(EXPERTS, dtype=jnp.int32)
    onehot = (flat_ids[:, :, None] == expert_range[None, None, :]).astype(jnp.int32)
    before = jnp.cumsum(onehot, axis=1) - onehot
    return jnp.sum(before * onehot, axis=2).astype(jnp.int32)


def reference(out_grad, normed, router, expert_ids, hidden_act, down_weight):
    groups = N_DP * N_TENSOR
    logits = jnp.dot(normed, router, preferred_element_type=jnp.float32)
    router_prob = jax.nn.softmax(logits, axis=-1)
    chosen = jnp.take_along_axis(router_prob, expert_ids, axis=1)
    gate_vals = (route_scale * chosen).astype(jnp.bfloat16)
    slot_rank = slot_ranks(expert_ids)
    source_ids = jnp.arange(groups, dtype=jnp.int32)[:, None]
    slot_rows = (expert_ids.reshape(groups, TOK_DEV * TOP) * (groups * CAP) + source_ids * CAP + slot_rank).reshape(-1)
    token_ids = (jnp.arange(TOKENS * TOP, dtype=jnp.int32) // TOP).astype(jnp.int32)
    total_rows = EXPERTS * groups * CAP
    token_of_row = jnp.full((total_rows,), TOKENS, jnp.int32).at[slot_rows].set(token_ids)
    gate_of_row = jnp.zeros((total_rows,), jnp.bfloat16).at[slot_rows].set(gate_vals.reshape(-1))
    padded = jnp.concatenate([out_grad, jnp.zeros((1, D), out_grad.dtype)], axis=0)

    def per_expert(expert_args):
        hidden_rows, weight, row_tokens, row_gates = expert_args
        incoming = padded[row_tokens]
        local_grad = (row_gates.astype(jnp.float32)[:, None] * incoming.astype(jnp.float32)).astype(jnp.bfloat16)
        expert_out = jnp.dot(hidden_rows, weight, preferred_element_type=jnp.float32)
        slot_score = jnp.sum(incoming.astype(jnp.float32) * expert_out, axis=1)
        grad_weight = jnp.dot(hidden_rows.T, local_grad, preferred_element_type=jnp.float32).astype(jnp.bfloat16)
        grad_hidden = jnp.dot(local_grad, weight.T, preferred_element_type=jnp.float32).astype(jnp.bfloat16)
        return grad_weight, grad_hidden, slot_score

    d_down, d_hidden, scores = lax.map(per_expert, (hidden_act, down_weight, token_of_row.reshape(EXPERTS, groups * CAP), gate_of_row.reshape(EXPERTS, groups * CAP)))
    gate_grad = scores.reshape(-1)[slot_rows].reshape(TOKENS, TOP)
    expert_range = jnp.arange(EXPERTS, dtype=jnp.int32)
    prob_grad = route_scale * jnp.sum(jnp.where(expert_ids[:, :, None] == expert_range[None, None, :], gate_grad[:, :, None], jnp.float32(0.0)), axis=1)
    logit_grad = (router_prob * (prob_grad - jnp.sum(router_prob * prob_grad, axis=1, keepdims=True))).astype(jnp.bfloat16)
    d_router = lax.dot_general(normed, logit_grad, (((0,), (0,)), ((), ())), preferred_element_type=jnp.float32)
    d_normed = jnp.dot(logit_grad, router.T, preferred_element_type=jnp.float32).astype(jnp.bfloat16)
    return d_down, d_hidden, d_router, d_normed
```

```python
import functools

import jax
import jax.numpy as jnp
from jax import lax
from jax.experimental import pallas as pl
from jax.experimental.pallas import tpu as pltpu
from jax.sharding import Mesh, PartitionSpec as P

route_scale = 16.0
ALL = ("dp", "z", "c")
CHIPS = ("dp", "z")
MIB = 1 << 20
NT = (((1,), (1,)), ((), ()))


def tile(size, best):
    return best if size % best == 0 else size


def route_kernel(capacity, ids_ref, grad_ref, rows_ref, code_ref, pick):
    @pl.when(pl.program_id(0) == 0)
    def _():
        experts, tokens = code_ref.shape
        expert = lax.broadcasted_iota(jnp.int32, (experts, tokens), 0)
        hit = ids_ref[0:1, :] == expert
        for k in range(1, ids_ref.shape[0]):
            hit = hit | (ids_ref[k : k + 1, :] == expert)
        earlier = lax.broadcasted_iota(jnp.int32, (tokens, tokens), 0)
        later = lax.broadcasted_iota(jnp.int32, (tokens, tokens), 1)
        before = jnp.where(earlier < later, 1.0, 0.0).astype(jnp.bfloat16)
        chosen = jnp.where(hit, 1.0, 0.0).astype(jnp.bfloat16)
        rank = jnp.dot(chosen, before, preferred_element_type=jnp.float32)
        code = jnp.where(hit, rank, -1.0)
        code_ref[...] = code
        slot = lax.broadcasted_iota(jnp.int32, (experts, capacity, tokens), 1).astype(jnp.float32)
        one = jnp.where(code[:, None, :] == slot, 1.0, 0.0)
        pick[...] = one.reshape(experts * capacity, tokens).astype(jnp.bfloat16)

    rows_ref[...] = jnp.dot(
        pick[...], grad_ref[...], preferred_element_type=jnp.float32
    ).astype(rows_ref.dtype)


def route(ids_t, out_grad, experts, capacity):
    tokens, width = out_grad.shape
    step = tile(width, 640)
    slots = experts * capacity
    return pl.pallas_call(
        functools.partial(route_kernel, capacity),
        grid=(width // step,),
        in_specs=[
            pl.BlockSpec(ids_t.shape, lambda i: (0, 0)),
            pl.BlockSpec((tokens, step), lambda i: (0, i)),
        ],
        out_specs=[
            pl.BlockSpec((slots, step), lambda i: (0, i)),
            pl.BlockSpec((experts, tokens), lambda i: (0, 0)),
        ],
        out_shape=[
            jax.ShapeDtypeStruct((slots, width), out_grad.dtype),
            jax.ShapeDtypeStruct((experts, tokens), jnp.float32),
        ],
        scratch_shapes=[pltpu.VMEM((slots, tokens), jnp.bfloat16)],
        compiler_params=pltpu.CompilerParams(vmem_limit_bytes=24 * MIB),
        cost_estimate=pl.CostEstimate(
            flops=2 * slots * tokens * width,
            bytes_accessed=2 * (slots + tokens) * width,
            transcendentals=0,
        ),
        name="route_rows",
    )(ids_t, out_grad)


def score_kernel(capacity, rows_ref, weight_ref, hidden_ref, gate_ref, dh_ref, score_ref, acc):
    step = pl.program_id(0)
    part = lax.dot_general(
        rows_ref[...], weight_ref[...], NT, preferred_element_type=jnp.float32
    )

    @pl.when(step == 0)
    def _():
        acc[...] = part

    @pl.when(step > 0)
    def _():
        acc[...] += part

    @pl.when(step == pl.num_programs(0) - 1)
    def _():
        slots = acc.shape[0]
        group = 2 * capacity
        total = acc[...]
        dh_ref[...] = (total * gate_ref[...]).astype(dh_ref.dtype)
        score = jnp.sum(total * hidden_ref[...].astype(jnp.float32), axis=1, keepdims=True)
        row = lax.broadcasted_iota(jnp.int32, (slots, 128), 0) % group
        lane = lax.broadcasted_iota(jnp.int32, (slots, 128), 1)
        spread = jnp.where(row == lane, score, 0.0)
        score_ref[...] = jnp.sum(spread.reshape(slots // group, group, 128), axis=1)


def scores(rows, weight, hidden, gate, capacity):
    slots, width = rows.shape
    units = weight.shape[0]
    step = tile(width, 512)
    return pl.pallas_call(
        functools.partial(score_kernel, capacity),
        grid=(width // step,),
        in_specs=[
            pl.BlockSpec((slots, step), lambda i: (0, i)),
            pl.BlockSpec((units, step), lambda i: (0, i)),
            pl.BlockSpec((slots, units), lambda i: (0, 0)),
            pl.BlockSpec((slots, 1), lambda i: (0, 0)),
        ],
        out_specs=[
            pl.BlockSpec((slots, units), lambda i: (0, 0)),
            pl.BlockSpec((slots // (2 * capacity), 128), lambda i: (0, 0)),
        ],
        out_shape=[
            jax.ShapeDtypeStruct((slots, units), jnp.bfloat16),
            jax.ShapeDtypeStruct((slots // (2 * capacity), 128), jnp.float32),
        ],
        scratch_shapes=[pltpu.VMEM((slots, units), jnp.float32)],
        compiler_params=pltpu.CompilerParams(vmem_limit_bytes=40 * MIB),
        cost_estimate=pl.CostEstimate(
            flops=2 * slots * units * width,
            bytes_accessed=2 * (slots + units) * width + 4 * slots * units,
            transcendentals=0,
        ),
        name="score_rows",
    )(rows, weight, hidden, gate)


def product_kernel(left_ref, right_ref, out_ref):
    out_ref[...] = jnp.dot(
        left_ref[...], right_ref[...], preferred_element_type=jnp.float32
    ).astype(out_ref.dtype)


def product(left, right, name):
    m, k = left.shape
    n = right.shape[1]
    step = tile(n, 512)
    return pl.pallas_call(
        product_kernel,
        grid=(n // step,),
        in_specs=[
            pl.BlockSpec((m, k), lambda i: (0, 0)),
            pl.BlockSpec((k, step), lambda i: (0, i)),
        ],
        out_specs=pl.BlockSpec((m, step), lambda i: (0, i)),
        out_shape=jax.ShapeDtypeStruct((m, n), jnp.bfloat16),
        compiler_params=pltpu.CompilerParams(vmem_limit_bytes=32 * MIB),
        cost_estimate=pl.CostEstimate(
            flops=2 * m * n * k, bytes_accessed=2 * (m * k + k * n + m * n), transcendentals=0
        ),
        name=name,
    )(left, right)


def router_kernel(capacity, back_ref, code_ref, prob_ref, normed_ref, terms_ref, grad_ref):
    halves, experts, tokens = code_ref.shape
    parts = []
    for half in range(halves):
        code = code_ref[half]
        prob = prob_ref[half]
        gate_grad = jnp.zeros((experts, tokens), jnp.float32)
        for r in range(capacity):
            at = half * capacity + r
            gate_grad = jnp.where(code == r, back_ref[:, at : at + 1], gate_grad)
        prob_grad = route_scale * gate_grad
        mean = jnp.sum(prob * prob_grad, axis=0, keepdims=True)
        parts.append(prob * (prob_grad - mean))
    grad = jnp.concatenate(parts, axis=1).astype(jnp.bfloat16)
    grad_ref[...] = grad
    terms_ref[...] = lax.dot_general(
        normed_ref[...], grad, NT, preferred_element_type=jnp.float32
    ).astype(terms_ref.dtype)


def router_terms(back, code, prob, normed_t, capacity):
    experts = back.shape[0]
    columns, tokens = normed_t.shape
    return pl.pallas_call(
        functools.partial(router_kernel, capacity),
        out_shape=[
            jax.ShapeDtypeStruct((columns, experts), jnp.bfloat16),
            jax.ShapeDtypeStruct((experts, tokens), jnp.bfloat16),
        ],
        compiler_params=pltpu.CompilerParams(vmem_limit_bytes=32 * MIB),
        cost_estimate=pl.CostEstimate(
            flops=2 * columns * experts * tokens,
            bytes_accessed=2 * columns * (experts + tokens),
            transcendentals=0,
        ),
        name="router_terms",
    )(back, code, prob, normed_t)


def all_to_all(x, axes):
    return lax.all_to_all(x, axes, split_axis=0, concat_axis=0, tiled=True)


def body(out_grad, normed, router, expert_ids, hidden_act, down_weight):
    groups = lax.axis_size(ALL)
    core = lax.axis_index("c")
    me = lax.axis_index(ALL)
    tokens, width = out_grad.shape
    experts = router.shape[1]
    hidden = hidden_act[0]
    weight = down_weight[0]
    capacity = hidden.shape[0] // groups
    slots = groups * capacity
    swap = [(0, 1), (1, 0)]

    send_rows, code_t = route(expert_ids.T, out_grad, experts, capacity)
    rows = all_to_all(send_rows.reshape(experts, capacity, width), ALL)
    rows = rows.reshape(slots, width)

    logits = jnp.dot(normed, router, preferred_element_type=jnp.float32)
    prob = jax.nn.softmax(logits, axis=-1)
    gates = (route_scale * prob).astype(jnp.bfloat16)
    code = code_t.T
    slot = jnp.arange(capacity, dtype=jnp.int32).astype(jnp.float32)
    slot_gate = jnp.sum(
        jnp.where(code[None] == slot[:, None, None], gates[None].astype(jnp.float32), 0.0), axis=1
    ).astype(jnp.bfloat16)
    all_gates = lax.all_gather(slot_gate, ALL, axis=0, tiled=False)
    mine = jnp.arange(experts, dtype=jnp.int32) == me
    gate = jnp.sum(jnp.where(mine, all_gates.astype(jnp.float32), 0.0), axis=2)
    gate = gate.reshape(slots, 1)
    gated_hidden_t = (gate * hidden.astype(jnp.float32)).astype(jnp.bfloat16).T

    own = jnp.stack([code_t, prob.T])
    other = lax.ppermute(own, "c", swap)
    first = core == 0
    pair = jnp.stack([jnp.where(first, own, other), jnp.where(first, other, own)], axis=1)
    halves = normed.T.reshape(groups // 2, 2, width // groups, tokens)
    keep = lax.dynamic_index_in_dim(halves, core, 1, keepdims=False)
    give = lax.dynamic_index_in_dim(halves, 1 - core, 1, keepdims=False)
    taken = lax.ppermute(give, "c", swap)
    pair_normed = jnp.where(
        first,
        jnp.concatenate([keep, taken], axis=2),
        jnp.concatenate([taken, keep], axis=2),
    ).reshape(width // 2, 2 * tokens)

    d_hidden, score = scores(rows, weight, hidden, gate, capacity)
    score = jnp.broadcast_to(score[:, None, :], (groups // 2, 2, 128)).reshape(groups, 128)
    back = all_to_all(score, ALL)
    d_down = product(gated_hidden_t, rows, "down_grad")

    terms, logit_grad_t = router_terms(back, pair[0], pair[1], pair_normed, capacity)
    got = all_to_all(terms.reshape(groups // 2, width // groups, experts), CHIPS)
    logit_grad = lax.dynamic_slice_in_dim(logit_grad_t, core * tokens, tokens, 1).T
    d_normed = lax.dot_general(
        logit_grad, router, NT, preferred_element_type=jnp.float32
    ).astype(jnp.bfloat16)
    d_router = jnp.sum(got.astype(jnp.float32), axis=0)
    return d_down[None], d_hidden[None], d_router, d_normed


def solution(mesh):
    dp, tensor = mesh.devices.shape
    fine = Mesh(mesh.devices.reshape(dp, tensor // 2, 2), ALL)
    in_specs = (
        P(ALL, None),
        P(ALL, None),
        P(),
        P(ALL, None),
        P(ALL, None, None),
        P(ALL, None, None),
    )
    out_specs = (P(ALL, None, None), P(ALL, None, None), P(ALL, None), P(ALL, None))
    return jax.shard_map(body, mesh=fine, in_specs=in_specs, out_specs=out_specs, check_vma=False)
```

```python
import functools

import jax
import jax.numpy as jnp
from jax import lax
from jax.experimental import pallas as pl
from jax.experimental.pallas import tpu as pltpu
from jax.sharding import Mesh, PartitionSpec as P

route_scale = 16.0
ALL = ("dp", "z", "c")
CHIPS = ("dp", "z")
MIB = 1 << 20
NT = (((1,), (1,)), ((), ()))
TN = (((0,), (0,)), ((), ()))


def cut(size, best):
    return best if size % best == 0 else size


def spread_columns(pick_ref, grad_ref, rows_hbm, rows, sem):
    width = rows.shape[1]
    step = cut(width, 512)
    copies = []
    for n in range(0, width, step):
        rows[:, n : n + step] = jnp.dot(
            pick_ref[...], grad_ref[:, n : n + step], preferred_element_type=jnp.float32
        ).astype(rows.dtype)
        columns = (slice(None), pl.ds(n, step))
        copy = pltpu.make_async_copy(rows.at[columns], rows_hbm.at[columns], sem.at[n // step])
        copy.start()
        copies.append(copy)
    for copy in copies:
        copy.wait()


def route_kernel(capacity, ids_ref, grad_ref, rows_hbm, code_ref, pick_ref, rows, sem):
    experts, tokens = code_ref.shape
    expert = lax.broadcasted_iota(jnp.int32, (experts, tokens), 0)
    hit = ids_ref[0:1, :] == expert
    for k in range(1, ids_ref.shape[0]):
        hit = hit | (ids_ref[k : k + 1, :] == expert)
    earlier = lax.broadcasted_iota(jnp.int32, (tokens, tokens), 0)
    later = lax.broadcasted_iota(jnp.int32, (tokens, tokens), 1)
    before = jnp.where(earlier < later, 1.0, 0.0).astype(jnp.bfloat16)
    chosen = jnp.where(hit, 1.0, 0.0).astype(jnp.bfloat16)
    rank = jnp.dot(chosen, before, preferred_element_type=jnp.float32)
    code = jnp.where(hit, rank, -1.0)
    code_ref[...] = code
    slot = lax.broadcasted_iota(jnp.int32, (experts, capacity, tokens), 1).astype(jnp.float32)
    one = jnp.where(code[:, None, :] == slot, 1.0, 0.0)
    pick_ref[...] = one.reshape(experts * capacity, tokens).astype(jnp.bfloat16)
    spread_columns(pick_ref, grad_ref, rows_hbm, rows, sem)


def route(ids_t, out_grad, experts, capacity, first, width):
    tokens = out_grad.shape[0]
    slots = experts * capacity
    return pl.pallas_call(
        functools.partial(route_kernel, capacity),
        grid=(1,),
        in_specs=[
            pl.BlockSpec(ids_t.shape, lambda i: (0, 0)),
            pl.BlockSpec((tokens, width), lambda i: (0, first // width)),
        ],
        out_specs=[
            pl.BlockSpec(memory_space=pl.ANY),
            pl.BlockSpec((experts, tokens), lambda i: (0, 0)),
            pl.BlockSpec((slots, tokens), lambda i: (0, 0)),
        ],
        out_shape=[
            jax.ShapeDtypeStruct((slots, width), out_grad.dtype),
            jax.ShapeDtypeStruct((experts, tokens), jnp.float32),
            jax.ShapeDtypeStruct((slots, tokens), jnp.bfloat16),
        ],
        scratch_shapes=[
            pltpu.VMEM((slots, width), out_grad.dtype),
            pltpu.SemaphoreType.DMA((width // cut(width, 512),)),
        ],
        compiler_params=pltpu.CompilerParams(vmem_limit_bytes=56 * MIB),
        cost_estimate=pl.CostEstimate(
            flops=2 * slots * tokens * width,
            bytes_accessed=2 * (slots + tokens) * width,
            transcendentals=0,
        ),
        name="route_rows",
    )(ids_t, out_grad)


def route_rest(pick, out_grad, first, width):
    slots, tokens = pick.shape
    return pl.pallas_call(
        spread_columns,
        grid=(1,),
        in_specs=[
            pl.BlockSpec((slots, tokens), lambda i: (0, 0)),
            pl.BlockSpec((tokens, width), lambda i: (0, first // width)),
        ],
        out_specs=pl.BlockSpec(memory_space=pl.ANY),
        out_shape=jax.ShapeDtypeStruct((slots, width), out_grad.dtype),
        scratch_shapes=[
            pltpu.VMEM((slots, width), out_grad.dtype),
            pltpu.SemaphoreType.DMA((width // cut(width, 512),)),
        ],
        compiler_params=pltpu.CompilerParams(vmem_limit_bytes=56 * MIB),
        cost_estimate=pl.CostEstimate(
            flops=2 * slots * tokens * width,
            bytes_accessed=2 * (slots + tokens) * width,
            transcendentals=0,
        ),
        name="route_rest",
    )(pick, out_grad)


def first_half_kernel(rows_ref, weight_ref, out_ref):
    part = lax.dot_general(
        rows_ref[...], weight_ref[...], NT, preferred_element_type=jnp.float32
    )

    @pl.when(pl.program_id(0) == 0)
    def _():
        out_ref[...] = part

    @pl.when(pl.program_id(0) > 0)
    def _():
        out_ref[...] += part


def first_half(rows, weight):
    slots, width = rows.shape
    units = weight.shape[0]
    step = cut(width, 1280)
    return pl.pallas_call(
        first_half_kernel,
        grid=(width // step,),
        in_specs=[
            pl.BlockSpec((slots, step), lambda i: (0, i)),
            pl.BlockSpec((units, step), lambda i: (0, i)),
        ],
        out_specs=pl.BlockSpec((slots, units), lambda i: (0, 0)),
        out_shape=jax.ShapeDtypeStruct((slots, units), jnp.float32),
        compiler_params=pltpu.CompilerParams(vmem_limit_bytes=40 * MIB),
        cost_estimate=pl.CostEstimate(
            flops=2 * slots * units * width,
            bytes_accessed=2 * (slots + units) * width + 4 * slots * units,
            transcendentals=0,
        ),
        name="first_half",
    )(rows, weight)


def score_kernel(
    capacity, rows_hbm, weight_hbm, hidden_hbm, half_hbm, gates_ref, proj_hbm, back_ref,
    rows, weight, hidden, half, proj, total, score, row_sem, weight_sem, proj_sem,
):
    slots, units = hidden.shape
    group = 2 * capacity
    width = rows.shape[1]
    bm, bn = cut(slots, 256), cut(units, 256)
    tall, wide = slots // bm, units // bn
    rest = pl.ds(weight_hbm.shape[1] - width, width)

    def load_rows(i):
        at = pl.ds(i * bm, bm)
        return [
            pltpu.make_async_copy(rows_hbm.at[at], rows.at[at], row_sem.at[0, i]),
            pltpu.make_async_copy(half_hbm.at[at], half.at[at], row_sem.at[1, i]),
            pltpu.make_async_copy(hidden_hbm.at[at], hidden.at[at], row_sem.at[2, i]),
        ]

    def load_weight(j):
        at = pl.ds(j * bn, bn)
        return [pltpu.make_async_copy(weight_hbm.at[at, rest], weight.at[at], weight_sem.at[j])]

    blocks = [(i / tall, 0, i) for i in range(tall)] + [(j / wide, 1, j) for j in range(wide)]
    blocks = sorted(blocks)
    loads = [load_weight(k) if kind else load_rows(k) for _, kind, k in blocks]
    for copies in loads[:3]:
        for copy in copies:
            copy.start()

    row = lax.broadcasted_iota(jnp.int32, (bm, 128), 0) % group
    lane = lax.broadcasted_iota(jnp.int32, (bm, 128), 1)
    stores = []
    have = ([], [])
    for step, (_, kind, k) in enumerate(blocks):
        for copy in loads[step]:
            copy.wait()
        if step + 3 < len(loads):
            for copy in loads[step + 3]:
                copy.start()
        have[kind].append(k)
        tiles = [(i, k) for i in have[0]] if kind else [(k, j) for j in have[1]]
        for i, j in tiles:
            at, to = slice(i * bm, (i + 1) * bm), slice(j * bn, (j + 1) * bn)
            part = half[at, to] + lax.dot_general(
                rows[at, :], weight[to, :], NT, preferred_element_type=jnp.float32
            )
            proj[at, to] = part.astype(proj.dtype)
            saved = hidden[at, to].astype(jnp.float32)
            part = jnp.sum(part * saved, axis=1, keepdims=True)
            total[at, :] = part if j == 0 else total[at, :] + part
            if j == wide - 1:
                block = pl.ds(i * bm, bm)
                store = pltpu.make_async_copy(proj.at[block], proj_hbm.at[block], proj_sem.at[i])
                store.start()
                stores.append(store)
                laid = jnp.where(row == lane, total[at, :], 0.0)
                score[i * bm // group : (i + 1) * bm // group, :] = jnp.sum(
                    laid.reshape(bm // group, group, 128), axis=1
                )
    both = score[...]
    chips = slots // group
    back_ref[pl.ds(0, chips, stride=2), :] = both
    back_ref[pl.ds(1, chips, stride=2), :] = both
    back_ref[...] += gates_ref[...]
    for store in stores:
        store.wait()


def scores(rows, weight, hidden, half, gates, capacity):
    slots, width = rows.shape
    units = weight.shape[0]
    bm, bn = cut(slots, 256), cut(units, 256)
    anywhere = pl.BlockSpec(memory_space=pl.ANY)
    inside = pl.BlockSpec(memory_space=pltpu.VMEM)
    return pl.pallas_call(
        functools.partial(score_kernel, capacity),
        in_specs=[anywhere, anywhere, anywhere, anywhere, inside],
        out_specs=[anywhere, inside],
        out_shape=[
            jax.ShapeDtypeStruct((slots, units), jnp.bfloat16),
            jax.ShapeDtypeStruct((slots // capacity, 128), jnp.float32),
        ],
        scratch_shapes=[
            pltpu.VMEM((slots, width), jnp.bfloat16),
            pltpu.VMEM((units, width), jnp.bfloat16),
            pltpu.VMEM((slots, units), jnp.bfloat16),
            pltpu.VMEM((slots, units), jnp.float32),
            pltpu.VMEM((slots, units), jnp.bfloat16),
            pltpu.VMEM((slots, 1), jnp.float32),
            pltpu.VMEM((slots // (2 * capacity), 128), jnp.float32),
            pltpu.SemaphoreType.DMA((3, slots // bm)),
            pltpu.SemaphoreType.DMA((units // bn,)),
            pltpu.SemaphoreType.DMA((slots // bm,)),
        ],
        compiler_params=pltpu.CompilerParams(vmem_limit_bytes=56 * MIB),
        cost_estimate=pl.CostEstimate(
            flops=2 * slots * units * width,
            bytes_accessed=2 * (slots + units) * width + 8 * slots * units,
            transcendentals=0,
        ),
        name="score_rows",
    )(rows, weight, hidden, half, gates)


def down_kernel(
    capacity, split, back_ref, hidden_ref, proj_ref, first_ref, second_ref, dw_ref, dh_ref, gated
):
    @pl.when(pl.program_id(0) == 0)
    def _():
        slots = hidden_ref.shape[0]
        groups = slots // capacity
        back = back_ref[...]
        slot = lax.broadcasted_iota(jnp.int32, (groups, capacity, 128), 1)
        lane = lax.broadcasted_iota(jnp.int32, (groups, capacity, 128), 2)
        own = jnp.where(lane == slot + 2 * capacity, back[:, None, :], 0.0)
        gate = jnp.sum(own.reshape(slots, 128), axis=1, keepdims=True)
        gated[...] = (gate * hidden_ref[...].astype(jnp.float32)).astype(gated.dtype)
        dh_ref[...] = (gate * proj_ref[...].astype(jnp.float32)).astype(dh_ref.dtype)

    def tile_of(rows_ref):
        dw_ref[...] = lax.dot_general(
            gated[...], rows_ref[...], TN, preferred_element_type=jnp.float32
        ).astype(dw_ref.dtype)

    @pl.when(pl.program_id(0) < split)
    def _():
        tile_of(first_ref)

    @pl.when(pl.program_id(0) >= split)
    def _():
        tile_of(second_ref)


def down_grads(back, hidden, proj, first, second, capacity):
    slots, units = hidden.shape
    width = first.shape[1] + second.shape[1]
    step = cut(first.shape[1], 1280)
    split = first.shape[1] // step
    whole = lambda i: (0, 0)
    return pl.pallas_call(
        functools.partial(down_kernel, capacity, split),
        grid=(width // step,),
        in_specs=[
            pl.BlockSpec(back.shape, whole),
            pl.BlockSpec(hidden.shape, whole),
            pl.BlockSpec(proj.shape, whole),
            pl.BlockSpec((slots, step), lambda i: (0, jnp.minimum(i, split - 1))),
            pl.BlockSpec((slots, step), lambda i: (0, jnp.maximum(i - split, 0))),
        ],
        out_specs=[
            pl.BlockSpec((units, step), lambda i: (0, i)),
            pl.BlockSpec((slots, units), whole),
        ],
        out_shape=[
            jax.ShapeDtypeStruct((units, width), jnp.bfloat16),
            jax.ShapeDtypeStruct((slots, units), jnp.bfloat16),
        ],
        scratch_shapes=[pltpu.VMEM((slots, units), jnp.bfloat16)],
        compiler_params=pltpu.CompilerParams(vmem_limit_bytes=56 * MIB),
        cost_estimate=pl.CostEstimate(
            flops=2 * slots * units * width,
            bytes_accessed=2 * (slots + units) * width + 6 * slots * units,
            transcendentals=0,
        ),
        name="down_grads",
    )(back, hidden, proj, first, second)


def router_kernel(capacity, back_ref, code_ref, prob_ref, normed_ref, terms_ref, grad_ref):
    halves, experts, tokens = code_ref.shape
    parts = []
    for half in range(halves):
        code = code_ref[half]
        prob = prob_ref[half]
        gate_grad = jnp.zeros((experts, tokens), jnp.float32)
        for r in range(capacity):
            at = half * capacity + r
            gate_grad = jnp.where(code == r, back_ref[:, at : at + 1], gate_grad)
        prob_grad = route_scale * gate_grad
        mean = jnp.sum(prob * prob_grad, axis=0, keepdims=True)
        parts.append(prob * (prob_grad - mean))
    grad = jnp.concatenate(parts, axis=1).astype(jnp.bfloat16)
    grad_ref[...] = grad
    terms_ref[...] = lax.dot_general(
        normed_ref[...], grad, NT, preferred_element_type=jnp.float32
    ).astype(terms_ref.dtype)


def router_terms(back, code, prob, normed_t, capacity):
    experts = back.shape[0]
    columns, tokens = normed_t.shape
    return pl.pallas_call(
        functools.partial(router_kernel, capacity),
        out_shape=[
            jax.ShapeDtypeStruct((columns, experts), jnp.bfloat16),
            jax.ShapeDtypeStruct((experts, tokens), jnp.bfloat16),
        ],
        compiler_params=pltpu.CompilerParams(vmem_limit_bytes=32 * MIB),
        cost_estimate=pl.CostEstimate(
            flops=2 * columns * experts * tokens,
            bytes_accessed=2 * columns * (experts + tokens),
            transcendentals=0,
        ),
        name="router_terms",
    )(back, code, prob, normed_t)


def all_to_all(x, axes):
    return lax.all_to_all(x, axes, split_axis=0, concat_axis=0, tiled=True)


def body(out_grad, normed, router, expert_ids, hidden_act, down_weight):
    groups = lax.axis_size(ALL)
    core = lax.axis_index("c")
    tokens, width = out_grad.shape
    experts = router.shape[1]
    hidden = hidden_act[0]
    weight = down_weight[0]
    capacity = hidden.shape[0] // groups
    slots = groups * capacity
    swap = [(0, 1), (1, 0)]

    part = width // 2
    send, code_t, pick = route(expert_ids.T, out_grad, experts, capacity, 0, part)
    first = all_to_all(send.reshape(experts, capacity, part), ALL).reshape(slots, part)
    send = route_rest(pick, out_grad, part, part)
    second = all_to_all(send.reshape(experts, capacity, part), ALL).reshape(slots, part)
    half = first_half(first, weight)

    logits = jnp.dot(normed, router, preferred_element_type=jnp.float32)
    prob = jax.nn.softmax(logits, axis=-1)
    gates = (route_scale * prob).astype(jnp.bfloat16)
    code = code_t.T
    slot = jnp.arange(capacity, dtype=jnp.int32).astype(jnp.float32)
    slot_gate = jnp.sum(
        jnp.where(code[None] == slot[:, None, None], gates[None].astype(jnp.float32), 0.0), axis=1
    ).astype(jnp.bfloat16)
    lanes = ((0, 0), (2 * capacity, 128 - 3 * capacity))
    gate_lanes = jnp.pad(slot_gate.astype(jnp.float32).T, lanes)

    own = jnp.stack([code_t, prob.T])
    other = lax.ppermute(own, "c", swap)
    even = core == 0
    pair = jnp.stack([jnp.where(even, own, other), jnp.where(even, other, own)], axis=1)
    halves = normed.T.reshape(groups // 2, 2, width // groups, tokens)
    keep = lax.dynamic_index_in_dim(halves, core, 1, keepdims=False)
    give = lax.dynamic_index_in_dim(halves, 1 - core, 1, keepdims=False)
    taken = lax.ppermute(give, "c", swap)
    pair_normed = jnp.where(
        even,
        jnp.concatenate([keep, taken], axis=2),
        jnp.concatenate([taken, keep], axis=2),
    ).reshape(width // 2, 2 * tokens)

    proj, score = scores(second, weight, hidden, half, gate_lanes, capacity)
    back = all_to_all(score, ALL)

    terms, logit_grad_t = router_terms(back, pair[0], pair[1], pair_normed, capacity)
    got = all_to_all(terms.reshape(groups // 2, width // groups, experts), CHIPS)
    d_down, d_hidden = down_grads(back, hidden, proj, first, second, capacity)
    logit_grad = lax.dynamic_slice_in_dim(logit_grad_t, core * tokens, tokens, 1).T
    d_normed = lax.dot_general(
        logit_grad, router, NT, preferred_element_type=jnp.float32
    ).astype(jnp.bfloat16)
    d_router = jnp.sum(got.astype(jnp.float32), axis=0)
    return d_down[None], d_hidden[None], d_router, d_normed


def solution(mesh):
    dp, tensor = mesh.devices.shape
    fine = Mesh(mesh.devices.reshape(dp, tensor // 2, 2), ALL)
    in_specs = (
        P(ALL, None),
        P(ALL, None),
        P(),
        P(ALL, None),
        P(ALL, None, None),
        P(ALL, None, None),
    )
    out_specs = (P(ALL, None, None), P(ALL, None, None), P(ALL, None), P(ALL, None))
    return jax.shard_map(body, mesh=fine, in_specs=in_specs, out_specs=out_specs, check_vma=False)
```

```python
import functools
import math

import jax
import jax.numpy as jnp
from jax import lax
from jax.experimental import pallas as pl
from jax.experimental.pallas import tpu as pltpu
from jax.sharding import Mesh, PartitionSpec as P

route_scale = 16.0
ALL = ("dp", "z", "c")
CHIPS = ("dp", "z")
MIB = 1 << 20
NT = (((1,), (1,)), ((), ()))


def cut(size, best):
    return best if size % best == 0 else size


def spread_columns(pick_ref, grad_ref, rows_hbm, rows, sem):
    width = rows.shape[1]
    step = cut(width, 256)
    copies = []
    for n in range(0, width, step):
        rows[:, n : n + step] = jnp.dot(
            pick_ref[...], grad_ref[:, n : n + step], preferred_element_type=jnp.float32
        ).astype(rows.dtype)
        columns = (slice(None), pl.ds(n, step))
        copy = pltpu.make_async_copy(rows.at[columns], rows_hbm.at[columns], sem.at[n // step])
        copy.start()
        copies.append(copy)
    for copy in copies:
        copy.wait()


def route_kernel(capacity, ids_ref, grad_ref, rows_hbm, code_ref, pick_ref, rows, sem):
    experts, tokens = code_ref.shape
    expert = lax.broadcasted_iota(jnp.int32, (experts, tokens), 0)
    hit = ids_ref[0:1, :] == expert
    for k in range(1, ids_ref.shape[0]):
        hit = hit | (ids_ref[k : k + 1, :] == expert)
    earlier = lax.broadcasted_iota(jnp.int32, (tokens, tokens), 0)
    later = lax.broadcasted_iota(jnp.int32, (tokens, tokens), 1)
    before = jnp.where(earlier < later, 1.0, 0.0).astype(jnp.bfloat16)
    chosen = jnp.where(hit, 1.0, 0.0).astype(jnp.bfloat16)
    rank = jnp.dot(chosen, before, preferred_element_type=jnp.float32)
    code = jnp.where(hit, rank, -1.0)
    code_ref[...] = code
    slot = lax.broadcasted_iota(jnp.int32, (experts, capacity, tokens), 1).astype(jnp.float32)
    one = jnp.where(code[:, None, :] == slot, 1.0, 0.0)
    pick_ref[...] = one.reshape(experts * capacity, tokens).astype(jnp.bfloat16)
    spread_columns(pick_ref, grad_ref, rows_hbm, rows, sem)


def route(ids_t, out_grad, experts, capacity, first, width):
    tokens = out_grad.shape[0]
    slots = experts * capacity
    return pl.pallas_call(
        functools.partial(route_kernel, capacity),
        grid=(1,),
        in_specs=[
            pl.BlockSpec(ids_t.shape, lambda i: (0, 0)),
            pl.BlockSpec((tokens, width), lambda i: (0, first // width)),
        ],
        out_specs=[
            pl.BlockSpec(memory_space=pl.ANY),
            pl.BlockSpec((experts, tokens), lambda i: (0, 0)),
            pl.BlockSpec((slots, tokens), lambda i: (0, 0)),
        ],
        out_shape=[
            jax.ShapeDtypeStruct((slots, width), out_grad.dtype),
            jax.ShapeDtypeStruct((experts, tokens), jnp.float32),
            jax.ShapeDtypeStruct((slots, tokens), jnp.bfloat16),
        ],
        scratch_shapes=[
            pltpu.VMEM((slots, width), out_grad.dtype),
            pltpu.SemaphoreType.DMA((width // cut(width, 256),)),
        ],
        compiler_params=pltpu.CompilerParams(vmem_limit_bytes=56 * MIB),
        cost_estimate=pl.CostEstimate(
            flops=2 * slots * tokens * width,
            bytes_accessed=2 * (slots + tokens) * width,
            transcendentals=0,
        ),
        name="route_rows",
    )(ids_t, out_grad)


def route_rest(pick, out_grad):
    slots, tokens = pick.shape
    width = out_grad.shape[1]
    return pl.pallas_call(
        spread_columns,
        grid=(1,),
        in_specs=[
            pl.BlockSpec((slots, tokens), lambda i: (0, 0)),
            pl.BlockSpec((tokens, width), lambda i: (0, 0)),
        ],
        out_specs=pl.BlockSpec(memory_space=pl.ANY),
        out_shape=jax.ShapeDtypeStruct((slots, width), out_grad.dtype),
        scratch_shapes=[
            pltpu.VMEM((slots, width), out_grad.dtype),
            pltpu.SemaphoreType.DMA((width // cut(width, 256),)),
        ],
        compiler_params=pltpu.CompilerParams(vmem_limit_bytes=56 * MIB),
        cost_estimate=pl.CostEstimate(
            flops=2 * slots * tokens * width,
            bytes_accessed=2 * (slots + tokens) * width,
            transcendentals=0,
        ),
        name="route_rest",
    )(pick, out_grad)


def project_kernel(start, rows_ref, weight_ref, *refs):
    out_ref, total = refs[-2:]
    part = lax.dot_general(
        rows_ref[...], weight_ref[...], NT, preferred_element_type=jnp.float32
    )

    @pl.when(pl.program_id(0) == 0)
    def _():
        total[...] = part + refs[0][...] if start else part

    @pl.when(pl.program_id(0) > 0)
    def _():
        total[...] += part

    @pl.when(pl.program_id(0) == pl.num_programs(0) - 1)
    def _():
        out_ref[...] = total[...].astype(out_ref.dtype)


def project(rows, weight, first, half, dtype, name):
    slots, width = rows.shape
    units = weight.shape[0]
    step = cut(math.gcd(width, first) if first else width, 1024)
    start = [] if half is None else [half]
    whole = lambda i: (0, 0)
    return pl.pallas_call(
        functools.partial(project_kernel, half is not None),
        grid=(width // step,),
        in_specs=[
            pl.BlockSpec((slots, step), lambda i: (0, i)),
            pl.BlockSpec((units, step), lambda i: (0, i + first // step)),
        ]
        + [pl.BlockSpec((slots, units), whole)] * len(start),
        out_specs=pl.BlockSpec((slots, units), whole),
        out_shape=jax.ShapeDtypeStruct((slots, units), dtype),
        scratch_shapes=[pltpu.VMEM((slots, units), jnp.float32)],
        compiler_params=pltpu.CompilerParams(vmem_limit_bytes=56 * MIB),
        cost_estimate=pl.CostEstimate(
            flops=2 * slots * units * width,
            bytes_accessed=2 * (slots + units) * width + 4 * slots * units,
            transcendentals=0,
        ),
        name=name,
    )(rows, weight, *start)


def score_kernel(
    capacity, rows_hbm, expert_hbm, partial_ref, gates_ref, back_ref, rows, expert, score, sem
):
    slots, width = rows.shape
    group = 2 * capacity
    bm = cut(slots, 128)
    loads = []
    for i in range(slots // bm):
        at = pl.ds(i * bm, bm)
        loads.append(
            [
                pltpu.make_async_copy(rows_hbm.at[at], rows.at[at], sem.at[0, i]),
                pltpu.make_async_copy(expert_hbm.at[at], expert.at[at], sem.at[1, i]),
            ]
        )
    ahead = 8
    for copies in loads[:ahead]:
        for copy in copies:
            copy.start()
    row = lax.broadcasted_iota(jnp.int32, (bm, 128), 0) % group
    lane = lax.broadcasted_iota(jnp.int32, (bm, 128), 1)
    for i, copies in enumerate(loads):
        for copy in copies:
            copy.wait()
        for copy in loads[i + ahead] if i + ahead < len(loads) else []:
            copy.start()
        at = slice(i * bm, (i + 1) * bm)
        total = partial_ref[at, :]
        for k in range(0, width, 128):
            total = total + rows[at, k : k + 128].astype(jnp.float32) * expert[
                at, k : k + 128
            ].astype(jnp.float32)
        total = jnp.sum(total, axis=1, keepdims=True)
        for core in range(2):
            laid = jnp.where((row + core * capacity) % group == lane, total, 0.0)
            score[core, i * bm // group : (i + 1) * bm // group, :] = jnp.sum(
                laid.reshape(bm // group, group, 128), axis=1
            )
    chips = slots // group
    back_ref[pl.ds(0, chips, stride=2), :] = score[0]
    back_ref[pl.ds(1, chips, stride=2), :] = score[1]
    back_ref[...] += gates_ref[...]


def partial_kernel(rows_ref, expert_ref, partial_ref):
    total = jnp.zeros(partial_ref.shape, jnp.float32)
    for k in range(0, rows_ref.shape[1], 128):
        total = total + rows_ref[:, k : k + 128].astype(jnp.float32) * expert_ref[
            :, k : k + 128
        ].astype(jnp.float32)
    partial_ref[...] = total


def partial_scores(rows, expert):
    slots, width = rows.shape
    bm = cut(slots, 128)
    return pl.pallas_call(
        partial_kernel,
        grid=(slots // bm,),
        in_specs=[pl.BlockSpec((bm, width), lambda i: (i, 0))] * 2,
        out_specs=pl.BlockSpec((bm, 128), lambda i: (i, 0)),
        out_shape=jax.ShapeDtypeStruct((slots, 128), jnp.float32),
        compiler_params=pltpu.CompilerParams(vmem_limit_bytes=24 * MIB),
        cost_estimate=pl.CostEstimate(
            flops=2 * slots * width, bytes_accessed=4 * slots * width, transcendentals=0
        ),
        name="partial_scores",
    )(rows, expert)


def scores(rows, expert, partial, gates, capacity):
    slots, width = rows.shape
    bm = cut(slots, 128)
    anywhere = pl.BlockSpec(memory_space=pl.ANY)
    inside = pl.BlockSpec(memory_space=pltpu.VMEM)
    return pl.pallas_call(
        functools.partial(score_kernel, capacity),
        in_specs=[anywhere, anywhere, inside, inside],
        out_specs=inside,
        out_shape=jax.ShapeDtypeStruct((slots // capacity, 128), jnp.float32),
        scratch_shapes=[
            pltpu.VMEM((slots, width), jnp.bfloat16),
            pltpu.VMEM((slots, width), jnp.bfloat16),
            pltpu.VMEM((2, slots // (2 * capacity), 128), jnp.float32),
            pltpu.SemaphoreType.DMA((2, slots // bm)),
        ],
        compiler_params=pltpu.CompilerParams(vmem_limit_bytes=56 * MIB),
        cost_estimate=pl.CostEstimate(
            flops=2 * slots * width, bytes_accessed=4 * slots * width, transcendentals=0
        ),
        name="score_rows",
    )(rows, expert, partial, gates)


def tiles(split, width):
    at = []
    n = 0
    while n < width:
        step = 512 if n == 0 or width - n <= 1024 else 1024
        step = min(step, (split if n < split else width) - n)
        at.append((n, step))
        n += step
    return at


def down_kernel(
    capacity, back_ref, grad_ref, hidden_hbm, proj_hbm, router_hbm, first_hbm, second_hbm,
    dw_hbm, dh_hbm, dn_hbm,
    hidden, proj, router, rows, gated, dw, dh, dn, in_sem, row_sem, dw_sem, out_sem,
):
    units, slots = hidden.shape
    split, width = first_hbm.shape[1], rows.shape[1]
    at = tiles(split, width)
    load_hidden = pltpu.make_async_copy(hidden_hbm, hidden, in_sem.at[0])
    load_proj = pltpu.make_async_copy(proj_hbm, proj, in_sem.at[1])
    load_router = pltpu.make_async_copy(router_hbm, router, in_sem.at[2])
    store_dh = pltpu.make_async_copy(dh, dh_hbm, out_sem.at[0])
    store_dn = pltpu.make_async_copy(dn, dn_hbm, out_sem.at[1])
    loads, stores = [], []
    for i, (n, step) in enumerate(at):
        columns = (slice(None), pl.ds(n, step))
        if n < split:
            source = first_hbm.at[columns]
        else:
            source = second_hbm.at[:, pl.ds(n - split, step)]
        loads.append(pltpu.make_async_copy(source, rows.at[columns], row_sem.at[i]))
        stores.append(pltpu.make_async_copy(dw.at[columns], dw_hbm.at[columns], dw_sem.at[i]))
    load_hidden.start()
    loads[0].start()

    groups = slots // capacity
    slot = lax.broadcasted_iota(jnp.int32, (groups, capacity, 128), 1)
    lane = lax.broadcasted_iota(jnp.int32, (groups, capacity, 128), 2)
    own = jnp.where(lane == slot + 2 * capacity, back_ref[...][:, None, :], 0.0)
    gate = jnp.sum(own.reshape(slots, 128), axis=1, keepdims=True)
    gate_row = jnp.broadcast_to(gate, (slots, 128)).T[0:1, :]
    load_hidden.wait()
    loads[1].start()
    gated[...] = (gate_row * hidden[...].astype(jnp.float32)).astype(gated.dtype)
    for i, (n, step) in enumerate(at):
        columns = slice(n, n + step)
        loads[i].wait()
        if i + 2 < len(loads):
            loads[i + 2].start()
        if i == 0:
            load_proj.start()
            load_router.start()
        dw[:, columns] = jnp.dot(
            gated[...], rows[:, columns], preferred_element_type=jnp.float32
        ).astype(dw.dtype)
        stores[i].start()
        if i == 1:
            load_proj.wait()
            dh[...] = (gate * proj[...].astype(jnp.float32)).astype(dh.dtype)
            store_dh.start()
            load_router.wait()
            grad = grad_ref[...].astype(jnp.float32).T.astype(jnp.bfloat16)
            dn[...] = lax.dot_general(
                grad, router[...], NT, preferred_element_type=jnp.float32
            ).astype(dn.dtype)
            store_dn.start()
    for store in stores:
        store.wait()
    store_dh.wait()
    store_dn.wait()


def down_grads(back, grad, hidden, proj, router, first, second, capacity):
    units, slots = hidden.shape
    split = first.shape[1]
    width = split + second.shape[1]
    experts, tokens = grad.shape
    count = len(tiles(split, width))
    anywhere = pl.BlockSpec(memory_space=pl.ANY)
    inside = pl.BlockSpec(memory_space=pltpu.VMEM)
    return pl.pallas_call(
        functools.partial(down_kernel, capacity),
        in_specs=[inside] * 2 + [anywhere] * 5,
        out_specs=[anywhere] * 3,
        out_shape=[
            jax.ShapeDtypeStruct((units, width), jnp.bfloat16),
            jax.ShapeDtypeStruct((slots, units), jnp.bfloat16),
            jax.ShapeDtypeStruct((tokens, width), jnp.bfloat16),
        ],
        scratch_shapes=[
            pltpu.VMEM((units, slots), jnp.bfloat16),
            pltpu.VMEM((slots, units), jnp.bfloat16),
            pltpu.VMEM((width, experts), jnp.bfloat16),
            pltpu.VMEM((slots, width), jnp.bfloat16),
            pltpu.VMEM((units, slots), jnp.bfloat16),
            pltpu.VMEM((units, width), jnp.bfloat16),
            pltpu.VMEM((slots, units), jnp.bfloat16),
            pltpu.VMEM((tokens, width), jnp.bfloat16),
            pltpu.SemaphoreType.DMA((3,)),
            pltpu.SemaphoreType.DMA((count,)),
            pltpu.SemaphoreType.DMA((count,)),
            pltpu.SemaphoreType.DMA((2,)),
        ],
        compiler_params=pltpu.CompilerParams(vmem_limit_bytes=56 * MIB),
        cost_estimate=pl.CostEstimate(
            flops=2 * slots * units * width + 2 * tokens * experts * width,
            bytes_accessed=2 * (slots + units + 2 * tokens) * width + 6 * slots * units,
            transcendentals=0,
        ),
        name="down_grads",
    )(back, grad, hidden, proj, router, first, second)


def router_kernel(
    capacity, back_ref, code_ref, prob_ref, other_code_ref, other_prob_ref, keep_ref, taken_ref,
    terms_ref, grad_ref,
):
    terms = None
    sides = ((code_ref, prob_ref, keep_ref), (other_code_ref, other_prob_ref, taken_ref))
    for side, (code, prob, normed) in enumerate(sides):
        code = code[...]
        prob = prob[...]
        gate_grad = jnp.zeros(code.shape, jnp.float32)
        for r in range(capacity):
            at = side * capacity + r
            gate_grad = jnp.where(code == r, back_ref[:, at : at + 1], gate_grad)
        prob_grad = route_scale * gate_grad
        mean = jnp.sum(prob * prob_grad, axis=0, keepdims=True)
        grad = (prob * (prob_grad - mean)).astype(jnp.bfloat16)
        if side == 0:
            grad_ref[...] = grad
        part = lax.dot_general(normed[...], grad, NT, preferred_element_type=jnp.float32)
        terms = part if side == 0 else terms + part
    terms_ref[...] = terms.astype(terms_ref.dtype)


def router_terms(back, own, other, keep, taken, capacity):
    experts = back.shape[0]
    columns, tokens = keep.shape
    return pl.pallas_call(
        functools.partial(router_kernel, capacity),
        out_shape=[
            jax.ShapeDtypeStruct((columns, experts), jnp.bfloat16),
            jax.ShapeDtypeStruct((experts, tokens), jnp.bfloat16),
        ],
        compiler_params=pltpu.CompilerParams(vmem_limit_bytes=32 * MIB),
        cost_estimate=pl.CostEstimate(
            flops=4 * columns * experts * tokens,
            bytes_accessed=4 * columns * (experts + tokens),
            transcendentals=0,
        ),
        name="router_terms",
    )(back, own[0], own[1], other[0], other[1], keep, taken)


def all_to_all(x, axes):
    return lax.all_to_all(x, axes, split_axis=0, concat_axis=0, tiled=True)


def body(out_grad, normed, router, expert_ids, hidden_act, down_weight):
    groups = lax.axis_size(ALL)
    core = lax.axis_index("c")
    tokens, width = out_grad.shape
    experts = router.shape[1]
    hidden = hidden_act[0]
    weight = down_weight[0]
    capacity = hidden.shape[0] // groups
    slots = groups * capacity
    swap = [(0, 1), (1, 0)]

    part = width * 3 // 5
    rest = width - part
    send, code_t, pick = route(expert_ids.T, out_grad, experts, capacity, 0, part)
    first = all_to_all(send.reshape(experts, capacity, part), ALL).reshape(slots, part)
    send = route_rest(pick, out_grad[:, part:])
    expert_out = [
        jnp.dot(hidden, w, preferred_element_type=jnp.float32).astype(jnp.bfloat16)
        for w in (weight[:, :part], weight[:, part:])
    ]
    send, expert_out, hidden_t = lax.optimization_barrier((send, expert_out, hidden.T))
    second = all_to_all(send.reshape(experts, capacity, rest), ALL).reshape(slots, rest)

    logits = jnp.dot(normed, router, preferred_element_type=jnp.float32)
    prob = jax.nn.softmax(logits, axis=-1)
    gates = (route_scale * prob).astype(jnp.bfloat16)
    code = code_t.T
    slot = jnp.arange(capacity, dtype=jnp.int32).astype(jnp.float32)
    slot_gate = jnp.sum(
        jnp.where(code[None] == slot[:, None, None], gates[None].astype(jnp.float32), 0.0), axis=1
    ).astype(jnp.bfloat16)
    lanes = ((0, 0), (2 * capacity, 128 - 3 * capacity))
    gate_lanes = jnp.pad(slot_gate.astype(jnp.float32).T, lanes)

    own = (code_t, prob.T)
    other = [lax.ppermute(x, "c", swap) for x in own]
    halves = normed.T.reshape(groups // 2, 2, width // groups, tokens)
    keep = lax.dynamic_index_in_dim(halves, core, 1, keepdims=False)
    give = lax.dynamic_index_in_dim(halves, 1 - core, 1, keepdims=False)
    taken = lax.ppermute(give, "c", swap).reshape(width // 2, tokens)
    keep = keep.reshape(width // 2, tokens)

    partial = partial_scores(first, expert_out[0])
    half = project(first, weight, 0, None, jnp.float32, "project_first")
    partial, half = lax.optimization_barrier((partial, half))

    score = scores(second, expert_out[1], partial, gate_lanes, capacity)
    back = all_to_all(score, ALL)
    proj = project(second, weight, part, half, jnp.bfloat16, "project_second")

    terms, logit_grad_t = router_terms(back, own, other, keep, taken, capacity)
    got = all_to_all(terms.reshape(groups // 2, width // groups, experts), CHIPS)
    d_down, d_hidden, d_normed = down_grads(
        back, logit_grad_t, hidden_t, proj, router, first, second, capacity
    )
    d_router = jnp.sum(got.astype(jnp.float32), axis=0)
    return d_down[None], d_hidden[None], d_router, d_normed


def solution(mesh):
    dp, tensor = mesh.devices.shape
    fine = Mesh(mesh.devices.reshape(dp, tensor // 2, 2), ALL)
    in_specs = (
        P(ALL, None),
        P(ALL, None),
        P(),
        P(ALL, None),
        P(ALL, None, None),
        P(ALL, None, None),
    )
    out_specs = (P(ALL, None, None), P(ALL, None, None), P(ALL, None), P(ALL, None))
    return jax.shard_map(body, mesh=fine, in_specs=in_specs, out_specs=out_specs, check_vma=False)
```

```python
import functools
import math

import jax
import jax.numpy as jnp
from jax import lax
from jax.experimental import pallas as pl
from jax.experimental.pallas import tpu as pltpu
from jax.sharding import Mesh, PartitionSpec as P

route_scale = 16.0
ALL = ("dp", "z", "c")
CHIPS = ("dp", "z")
MIB = 1 << 20
NT = (((1,), (1,)), ((), ()))


def cut(size, best):
    return best if size % best == 0 else size


def spread_columns(pick, load, grad, rows, rows_hbm, sem):
    width = rows.shape[1]
    step = cut(width, 512)
    copies = []
    for n in range(0, width, step):
        load(n, step)
        rows[:, n : n + step] = jnp.dot(
            pick[...], grad[:, n : n + step], preferred_element_type=jnp.float32
        ).astype(rows.dtype)
        columns = (slice(None), pl.ds(n, step))
        copy = pltpu.make_async_copy(rows.at[columns], rows_hbm.at[columns], sem.at[n // step])
        copy.start()
        copies.append(copy)
    for copy in copies:
        copy.wait()


def route_kernel(
    capacity, ids_ref, grad_hbm, rows_hbm, code_hbm, pick_hbm,
    grad, rows, code_ref, pick, load_sem, sem, save_sem,
):
    width = rows.shape[1]
    half = width // 2
    loads = [
        pltpu.make_async_copy(
            grad_hbm.at[:, pl.ds(n, half)], grad.at[:, pl.ds(n, half)], load_sem.at[n // half]
        )
        for n in (0, half)
    ]
    for copy in loads:
        copy.start()
    experts, tokens = code_ref.shape
    expert = lax.broadcasted_iota(jnp.int32, (experts, tokens), 0)
    hit = ids_ref[0:1, :] == expert
    for k in range(1, ids_ref.shape[0]):
        hit = hit | (ids_ref[k : k + 1, :] == expert)
    earlier = lax.broadcasted_iota(jnp.int32, (tokens, tokens), 0)
    later = lax.broadcasted_iota(jnp.int32, (tokens, tokens), 1)
    before = jnp.where(earlier < later, 1.0, 0.0).astype(jnp.bfloat16)
    chosen = jnp.where(hit, 1.0, 0.0).astype(jnp.bfloat16)
    rank = jnp.dot(chosen, before, preferred_element_type=jnp.float32)
    code = jnp.where(hit, rank, -1.0)
    code_ref[...] = code
    slot = lax.broadcasted_iota(jnp.int32, (experts, capacity, tokens), 1).astype(jnp.float32)
    one = jnp.where(code[:, None, :] == slot, 1.0, 0.0)
    pick[...] = one.reshape(experts * capacity, tokens).astype(jnp.bfloat16)
    saves = [
        pltpu.make_async_copy(code_ref, code_hbm, save_sem.at[0]),
        pltpu.make_async_copy(pick, pick_hbm, save_sem.at[1]),
    ]
    for copy in saves:
        copy.start()

    def load(n, step):
        if n == 0:
            loads[0].wait()
        if n < half <= n + step - 1 or n == half:
            loads[1].wait()

    spread_columns(pick, load, grad, rows, rows_hbm, sem)
    for copy in saves:
        copy.wait()


def route(ids_t, out_grad, experts, capacity, width):
    tokens = out_grad.shape[0]
    slots = experts * capacity
    anywhere = pl.BlockSpec(memory_space=pl.ANY)
    return pl.pallas_call(
        functools.partial(route_kernel, capacity),
        in_specs=[pl.BlockSpec(memory_space=pltpu.VMEM), anywhere],
        out_specs=[anywhere] * 3,
        out_shape=[
            jax.ShapeDtypeStruct((slots, width), out_grad.dtype),
            jax.ShapeDtypeStruct((experts, tokens), jnp.float32),
            jax.ShapeDtypeStruct((slots, tokens), jnp.bfloat16),
        ],
        scratch_shapes=[
            pltpu.VMEM((tokens, width), out_grad.dtype),
            pltpu.VMEM((slots, width), out_grad.dtype),
            pltpu.VMEM((experts, tokens), jnp.float32),
            pltpu.VMEM((slots, tokens), jnp.bfloat16),
            pltpu.SemaphoreType.DMA((2,)),
            pltpu.SemaphoreType.DMA((width // cut(width, 512),)),
            pltpu.SemaphoreType.DMA((2,)),
        ],
        compiler_params=pltpu.CompilerParams(vmem_limit_bytes=56 * MIB),
        cost_estimate=pl.CostEstimate(
            flops=2 * slots * tokens * width,
            bytes_accessed=2 * (slots + tokens) * width,
            transcendentals=0,
        ),
        name="route_rows",
    )(ids_t, out_grad)


def rest_kernel(pick_ref, grad_ref, rows_hbm, rows, sem):
    spread_columns(pick_ref, lambda n, step: None, grad_ref, rows, rows_hbm, sem)


def route_rest(pick, out_grad):
    slots, tokens = pick.shape
    width = out_grad.shape[1]
    return pl.pallas_call(
        rest_kernel,
        grid=(1,),
        in_specs=[
            pl.BlockSpec((slots, tokens), lambda i: (0, 0)),
            pl.BlockSpec((tokens, width), lambda i: (0, 0)),
        ],
        out_specs=pl.BlockSpec(memory_space=pl.ANY),
        out_shape=jax.ShapeDtypeStruct((slots, width), out_grad.dtype),
        scratch_shapes=[
            pltpu.VMEM((slots, width), out_grad.dtype),
            pltpu.SemaphoreType.DMA((width // cut(width, 512),)),
        ],
        compiler_params=pltpu.CompilerParams(vmem_limit_bytes=56 * MIB),
        cost_estimate=pl.CostEstimate(
            flops=2 * slots * tokens * width,
            bytes_accessed=2 * (slots + tokens) * width,
            transcendentals=0,
        ),
        name="route_rest",
    )(pick, out_grad)


def project_kernel(start, rows_ref, weight_ref, *refs):
    if start:
        half_hbm, out_ref, total, half, sem = refs
        load = pltpu.make_async_copy(half_hbm, half, sem)
    else:
        out_ref, total = refs

    @pl.when(pl.program_id(0) == 0)
    def _():
        if start:
            load.start()
        total[...] = lax.dot_general(
            rows_ref[...], weight_ref[...], NT, preferred_element_type=jnp.float32
        )

    @pl.when(pl.program_id(0) > 0)
    def _():
        total[...] += lax.dot_general(
            rows_ref[...], weight_ref[...], NT, preferred_element_type=jnp.float32
        )

    @pl.when(pl.program_id(0) == pl.num_programs(0) - 1)
    def _():
        if start:
            load.wait()
            out_ref[...] = (total[...] + half[...]).astype(out_ref.dtype)
        else:
            out_ref[...] = total[...].astype(out_ref.dtype)


def project(rows, weight, first, half, dtype, name):
    slots, width = rows.shape
    units = weight.shape[0]
    step = cut(math.gcd(width, first) if first else width, 1024)
    start = [] if half is None else [half]
    total = pltpu.VMEM((slots, units), jnp.float32)
    return pl.pallas_call(
        functools.partial(project_kernel, half is not None),
        grid=(width // step,),
        in_specs=[
            pl.BlockSpec((slots, step), lambda i: (0, i)),
            pl.BlockSpec((units, step), lambda i: (0, i + first // step)),
        ]
        + [pl.BlockSpec(memory_space=pl.ANY)] * len(start),
        out_specs=pl.BlockSpec((slots, units), lambda i: (0, 0)),
        out_shape=jax.ShapeDtypeStruct((slots, units), dtype),
        scratch_shapes=[total] + [total, pltpu.SemaphoreType.DMA(())] * len(start),
        compiler_params=pltpu.CompilerParams(vmem_limit_bytes=56 * MIB),
        cost_estimate=pl.CostEstimate(
            flops=2 * slots * units * width,
            bytes_accessed=2 * (slots + units) * width + 4 * slots * units,
            transcendentals=0,
        ),
        name=name,
    )(rows, weight, *start)


def score_kernel(
    capacity, rows_hbm, expert_hbm, partial_ref, gates_ref, back_ref, rows, expert, score, sem
):
    slots, width = rows.shape
    group = 2 * capacity
    bm = cut(slots, 128)
    loads = []
    for i in range(slots // bm):
        at = pl.ds(i * bm, bm)
        loads.append(
            [
                pltpu.make_async_copy(rows_hbm.at[at], rows.at[at], sem.at[0, i]),
                pltpu.make_async_copy(expert_hbm.at[at], expert.at[at], sem.at[1, i]),
            ]
        )
    ahead = 8
    for copies in loads[:ahead]:
        for copy in copies:
            copy.start()
    row = lax.broadcasted_iota(jnp.int32, (bm, 128), 0) % group
    lane = lax.broadcasted_iota(jnp.int32, (bm, 128), 1)
    for i, copies in enumerate(loads):
        for copy in copies:
            copy.wait()
        for copy in loads[i + ahead] if i + ahead < len(loads) else []:
            copy.start()
        at = slice(i * bm, (i + 1) * bm)
        total = partial_ref[at, :]
        for k in range(0, width, 128):
            total = total + rows[at, k : k + 128].astype(jnp.float32) * expert[
                at, k : k + 128
            ].astype(jnp.float32)
        total = jnp.sum(total, axis=1, keepdims=True)
        for core in range(2):
            laid = jnp.where((row + core * capacity) % group == lane, total, 0.0)
            score[core, i * bm // group : (i + 1) * bm // group, :] = jnp.sum(
                laid.reshape(bm // group, group, 128), axis=1
            )
    chips = slots // group
    back_ref[pl.ds(0, chips, stride=2), :] = score[0]
    back_ref[pl.ds(1, chips, stride=2), :] = score[1]
    back_ref[...] += gates_ref[...]


def partial_kernel(rows_ref, expert_ref, partial_ref):
    total = jnp.zeros(partial_ref.shape, jnp.float32)
    for k in range(0, rows_ref.shape[1], 128):
        total = total + rows_ref[:, k : k + 128].astype(jnp.float32) * expert_ref[
            :, k : k + 128
        ].astype(jnp.float32)
    partial_ref[...] = total


def partial_scores(rows, expert):
    slots, width = rows.shape
    bm = cut(slots, 128)
    return pl.pallas_call(
        partial_kernel,
        grid=(slots // bm,),
        in_specs=[pl.BlockSpec((bm, width), lambda i: (i, 0))] * 2,
        out_specs=pl.BlockSpec((bm, 128), lambda i: (i, 0)),
        out_shape=jax.ShapeDtypeStruct((slots, 128), jnp.float32),
        compiler_params=pltpu.CompilerParams(vmem_limit_bytes=24 * MIB),
        cost_estimate=pl.CostEstimate(
            flops=2 * slots * width, bytes_accessed=4 * slots * width, transcendentals=0
        ),
        name="partial_scores",
    )(rows, expert)


def scores(rows, expert, partial, gates, capacity):
    slots, width = rows.shape
    bm = cut(slots, 128)
    anywhere = pl.BlockSpec(memory_space=pl.ANY)
    inside = pl.BlockSpec(memory_space=pltpu.VMEM)
    return pl.pallas_call(
        functools.partial(score_kernel, capacity),
        in_specs=[anywhere, anywhere, inside, inside],
        out_specs=inside,
        out_shape=jax.ShapeDtypeStruct((slots // capacity, 128), jnp.float32),
        scratch_shapes=[
            pltpu.VMEM((slots, width), jnp.bfloat16),
            pltpu.VMEM((slots, width), jnp.bfloat16),
            pltpu.VMEM((2, slots // (2 * capacity), 128), jnp.float32),
            pltpu.SemaphoreType.DMA((2, slots // bm)),
        ],
        compiler_params=pltpu.CompilerParams(vmem_limit_bytes=56 * MIB),
        cost_estimate=pl.CostEstimate(
            flops=2 * slots * width, bytes_accessed=4 * slots * width, transcendentals=0
        ),
        name="score_rows",
    )(rows, expert, partial, gates)


def tiles(split, width):
    at = []
    n = 0
    while n < width:
        step = 512 if n == 0 or width - n <= 1024 else 1024
        step = min(step, (split if n < split else width) - n)
        at.append((n, step))
        n += step
    return at


def down_kernel(
    capacity, back_ref, grad_ref, hidden_hbm, proj_hbm, router_hbm, first_hbm, second_hbm,
    dw_hbm, dh_hbm, dn_hbm,
    hidden, proj, router, rows, gated, dw, dh, dn, in_sem, row_sem, dw_sem, out_sem,
):
    units, slots = hidden.shape
    split, width = first_hbm.shape[1], rows.shape[1]
    at = tiles(split, width)
    load_hidden = pltpu.make_async_copy(hidden_hbm, hidden, in_sem.at[0])
    load_proj = pltpu.make_async_copy(proj_hbm, proj, in_sem.at[1])
    load_router = pltpu.make_async_copy(router_hbm, router, in_sem.at[2])
    store_dh = pltpu.make_async_copy(dh, dh_hbm, out_sem.at[0])
    store_dn = pltpu.make_async_copy(dn, dn_hbm, out_sem.at[1])
    loads, stores = [], []
    for i, (n, step) in enumerate(at):
        columns = (slice(None), pl.ds(n, step))
        if n < split:
            source = first_hbm.at[columns]
        else:
            source = second_hbm.at[:, pl.ds(n - split, step)]
        loads.append(pltpu.make_async_copy(source, rows.at[columns], row_sem.at[i]))
        stores.append(pltpu.make_async_copy(dw.at[columns], dw_hbm.at[columns], dw_sem.at[i]))
    load_hidden.start()
    loads[0].start()

    groups = slots // capacity
    slot = lax.broadcasted_iota(jnp.int32, (groups, capacity, 128), 1)
    lane = lax.broadcasted_iota(jnp.int32, (groups, capacity, 128), 2)
    own = jnp.where(lane == slot + 2 * capacity, back_ref[...][:, None, :], 0.0)
    gate = jnp.sum(own.reshape(slots, 128), axis=1, keepdims=True)
    gate_row = jnp.broadcast_to(gate, (slots, 128)).T[0:1, :]
    load_hidden.wait()
    loads[1].start()
    gated[...] = (gate_row * hidden[...].astype(jnp.float32)).astype(gated.dtype)
    for i, (n, step) in enumerate(at):
        columns = slice(n, n + step)
        loads[i].wait()
        if i + 2 < len(loads):
            loads[i + 2].start()
        if i == 0:
            load_proj.start()
            load_router.start()
        dw[:, columns] = jnp.dot(
            gated[...], rows[:, columns], preferred_element_type=jnp.float32
        ).astype(dw.dtype)
        stores[i].start()
        if i == 1:
            load_proj.wait()
            dh[...] = (gate * proj[...].astype(jnp.float32)).astype(dh.dtype)
            store_dh.start()
            load_router.wait()
            grad = grad_ref[...].astype(jnp.float32).T.astype(jnp.bfloat16)
            dn[...] = lax.dot_general(
                grad, router[...], NT, preferred_element_type=jnp.float32
            ).astype(dn.dtype)
            store_dn.start()
    for store in stores:
        store.wait()
    store_dh.wait()
    store_dn.wait()


def down_grads(back, grad, hidden, proj, router, first, second, capacity):
    units, slots = hidden.shape
    split = first.shape[1]
    width = split + second.shape[1]
    experts, tokens = grad.shape
    count = len(tiles(split, width))
    anywhere = pl.BlockSpec(memory_space=pl.ANY)
    inside = pl.BlockSpec(memory_space=pltpu.VMEM)
    return pl.pallas_call(
        functools.partial(down_kernel, capacity),
        in_specs=[inside] * 2 + [anywhere] * 5,
        out_specs=[anywhere] * 3,
        out_shape=[
            jax.ShapeDtypeStruct((units, width), jnp.bfloat16),
            jax.ShapeDtypeStruct((slots, units), jnp.bfloat16),
            jax.ShapeDtypeStruct((tokens, width), jnp.bfloat16),
        ],
        scratch_shapes=[
            pltpu.VMEM((units, slots), jnp.bfloat16),
            pltpu.VMEM((slots, units), jnp.bfloat16),
            pltpu.VMEM((width, experts), jnp.bfloat16),
            pltpu.VMEM((slots, width), jnp.bfloat16),
            pltpu.VMEM((units, slots), jnp.bfloat16),
            pltpu.VMEM((units, width), jnp.bfloat16),
            pltpu.VMEM((slots, units), jnp.bfloat16),
            pltpu.VMEM((tokens, width), jnp.bfloat16),
            pltpu.SemaphoreType.DMA((3,)),
            pltpu.SemaphoreType.DMA((count,)),
            pltpu.SemaphoreType.DMA((count,)),
            pltpu.SemaphoreType.DMA((2,)),
        ],
        compiler_params=pltpu.CompilerParams(vmem_limit_bytes=56 * MIB),
        cost_estimate=pl.CostEstimate(
            flops=2 * slots * units * width + 2 * tokens * experts * width,
            bytes_accessed=2 * (slots + units + 2 * tokens) * width + 6 * slots * units,
            transcendentals=0,
        ),
        name="down_grads",
    )(back, grad, hidden, proj, router, first, second)


def router_kernel(
    capacity, back_ref, code_ref, prob_ref, other_code_ref, other_prob_ref, keep_ref, taken_ref,
    terms_ref, grad_ref,
):
    terms = None
    sides = ((code_ref, prob_ref, keep_ref), (other_code_ref, other_prob_ref, taken_ref))
    for side, (code, prob, normed) in enumerate(sides):
        code = code[...]
        prob = prob[...]
        gate_grad = jnp.zeros(code.shape, jnp.float32)
        for r in range(capacity):
            at = side * capacity + r
            gate_grad = jnp.where(code == r, back_ref[:, at : at + 1], gate_grad)
        prob_grad = route_scale * gate_grad
        mean = jnp.sum(prob * prob_grad, axis=0, keepdims=True)
        grad = (prob * (prob_grad - mean)).astype(jnp.bfloat16)
        if side == 0:
            grad_ref[...] = grad
        part = lax.dot_general(normed[...], grad, NT, preferred_element_type=jnp.float32)
        terms = part if side == 0 else terms + part
    terms_ref[...] = terms.astype(terms_ref.dtype)


def router_terms(back, own, other, keep, taken, capacity):
    experts = back.shape[0]
    columns, tokens = keep.shape
    return pl.pallas_call(
        functools.partial(router_kernel, capacity),
        out_shape=[
            jax.ShapeDtypeStruct((columns, experts), jnp.bfloat16),
            jax.ShapeDtypeStruct((experts, tokens), jnp.bfloat16),
        ],
        compiler_params=pltpu.CompilerParams(vmem_limit_bytes=32 * MIB),
        cost_estimate=pl.CostEstimate(
            flops=4 * columns * experts * tokens,
            bytes_accessed=4 * columns * (experts + tokens),
            transcendentals=0,
        ),
        name="router_terms",
    )(back, own[0], own[1], other[0], other[1], keep, taken)


def all_to_all(x, axes):
    return lax.all_to_all(x, axes, split_axis=0, concat_axis=0, tiled=True)


def body(out_grad, normed, router, expert_ids, hidden_act, down_weight):
    groups = lax.axis_size(ALL)
    core = lax.axis_index("c")
    tokens, width = out_grad.shape
    experts = router.shape[1]
    hidden = hidden_act[0]
    weight = down_weight[0]
    capacity = hidden.shape[0] // groups
    slots = groups * capacity
    swap = [(0, 1), (1, 0)]

    part = width * 3 // 5
    rest = width - part
    send, code_t, pick = route(expert_ids.T, out_grad, experts, capacity, part)
    first = all_to_all(send.reshape(experts, capacity, part), ALL).reshape(slots, part)
    send = route_rest(pick, out_grad[:, part:])
    expert_out = [
        jnp.dot(hidden, w, preferred_element_type=jnp.float32).astype(jnp.bfloat16)
        for w in (weight[:, :part], weight[:, part:])
    ]
    send, expert_out, hidden_t = lax.optimization_barrier((send, expert_out, hidden.T))
    second = all_to_all(send.reshape(experts, capacity, rest), ALL).reshape(slots, rest)

    logits = jnp.dot(normed, router, preferred_element_type=jnp.float32)
    prob = jax.nn.softmax(logits, axis=-1)
    gates = (route_scale * prob).astype(jnp.bfloat16)
    code = code_t.T
    slot = jnp.arange(capacity, dtype=jnp.int32).astype(jnp.float32)
    slot_gate = jnp.sum(
        jnp.where(code[None] == slot[:, None, None], gates[None].astype(jnp.float32), 0.0), axis=1
    ).astype(jnp.bfloat16)
    lanes = ((0, 0), (2 * capacity, 128 - 3 * capacity))
    gate_lanes = jnp.pad(slot_gate.astype(jnp.float32).T, lanes)

    own = (code_t, prob.T)
    other = [lax.ppermute(x, "c", swap) for x in own]
    halves = normed.T.reshape(groups // 2, 2, width // groups, tokens)
    keep = lax.dynamic_index_in_dim(halves, core, 1, keepdims=False)
    give = lax.dynamic_index_in_dim(halves, 1 - core, 1, keepdims=False)
    taken = lax.ppermute(give, "c", swap).reshape(width // 2, tokens)
    keep = keep.reshape(width // 2, tokens)

    partial = partial_scores(first, expert_out[0])
    half = project(first, weight, 0, None, jnp.float32, "project_first")
    partial, half = lax.optimization_barrier((partial, half))

    score = scores(second, expert_out[1], partial, gate_lanes, capacity)
    back = all_to_all(score, ALL)
    proj = project(second, weight, part, half, jnp.bfloat16, "project_second")

    terms, logit_grad_t = router_terms(back, own, other, keep, taken, capacity)
    got = all_to_all(terms.reshape(groups // 2, width // groups, experts), CHIPS)
    d_down, d_hidden, d_normed = down_grads(
        back, logit_grad_t, hidden_t, proj, router, first, second, capacity
    )
    d_router = jnp.sum(got.astype(jnp.float32), axis=0)
    return d_down[None], d_hidden[None], d_router, d_normed


def solution(mesh):
    dp, tensor = mesh.devices.shape
    fine = Mesh(mesh.devices.reshape(dp, tensor // 2, 2), ALL)
    in_specs = (
        P(ALL, None),
        P(ALL, None),
        P(),
        P(ALL, None),
        P(ALL, None, None),
        P(ALL, None, None),
    )
    out_specs = (P(ALL, None, None), P(ALL, None, None), P(ALL, None), P(ALL, None))
    return jax.shard_map(body, mesh=fine, in_specs=in_specs, out_specs=out_specs, check_vma=False)
```

```python
import functools
import math

import jax
import jax.numpy as jnp
from jax import lax
from jax.experimental import pallas as pl
from jax.experimental.pallas import tpu as pltpu
from jax.sharding import Mesh, PartitionSpec as P

route_scale = 16.0
ALL = ("dp", "z", "c")
CHIPS = ("dp", "z")
MIB = 1 << 20
NT = (((1,), (1,)), ((), ()))


def cut(size, best):
    return best if size % best == 0 else size


def spread_columns(pick, load, grad, rows, rows_hbm, sem):
    width = rows.shape[1]
    step = cut(width, 512)
    copies = []
    for n in range(0, width, step):
        load(n, step)
        rows[:, n : n + step] = jnp.dot(
            pick[...], grad[:, n : n + step], preferred_element_type=jnp.float32
        ).astype(rows.dtype)
        columns = (slice(None), pl.ds(n, step))
        copy = pltpu.make_async_copy(rows.at[columns], rows_hbm.at[columns], sem.at[n // step])
        copy.start()
        copies.append(copy)
    for copy in copies:
        copy.wait()


def route_kernel(
    capacity, ids_ref, grad_hbm, rows_hbm, code_hbm, pick_hbm,
    grad, rows, code_ref, pick, load_sem, sem, save_sem,
):
    width = rows.shape[1]
    half = width // 2
    loads = [
        pltpu.make_async_copy(
            grad_hbm.at[:, pl.ds(n, half)], grad.at[:, pl.ds(n, half)], load_sem.at[n // half]
        )
        for n in (0, half)
    ]
    for copy in loads:
        copy.start()
    experts, tokens = code_ref.shape
    expert = lax.broadcasted_iota(jnp.int32, (experts, tokens), 0)
    hit = ids_ref[0:1, :] == expert
    for k in range(1, ids_ref.shape[0]):
        hit = hit | (ids_ref[k : k + 1, :] == expert)
    earlier = lax.broadcasted_iota(jnp.int32, (tokens, tokens), 0)
    later = lax.broadcasted_iota(jnp.int32, (tokens, tokens), 1)
    before = jnp.where(earlier < later, 1.0, 0.0).astype(jnp.bfloat16)
    chosen = jnp.where(hit, 1.0, 0.0).astype(jnp.bfloat16)
    rank = jnp.dot(chosen, before, preferred_element_type=jnp.float32)
    code = jnp.where(hit, rank, -1.0)
    code_ref[...] = code
    slot = lax.broadcasted_iota(jnp.int32, (experts, capacity, tokens), 1).astype(jnp.float32)
    one = jnp.where(code[:, None, :] == slot, 1.0, 0.0)
    pick[...] = one.reshape(experts * capacity, tokens).astype(jnp.bfloat16)
    saves = [
        pltpu.make_async_copy(code_ref, code_hbm, save_sem.at[0]),
        pltpu.make_async_copy(pick, pick_hbm, save_sem.at[1]),
    ]
    for copy in saves:
        copy.start()

    def load(n, step):
        if n == 0:
            loads[0].wait()
        if n < half <= n + step - 1 or n == half:
            loads[1].wait()

    spread_columns(pick, load, grad, rows, rows_hbm, sem)
    for copy in saves:
        copy.wait()


def route(ids_t, out_grad, experts, capacity, width):
    tokens = out_grad.shape[0]
    slots = experts * capacity
    anywhere = pl.BlockSpec(memory_space=pl.ANY)
    return pl.pallas_call(
        functools.partial(route_kernel, capacity),
        in_specs=[pl.BlockSpec(memory_space=pltpu.VMEM), anywhere],
        out_specs=[anywhere] * 3,
        out_shape=[
            jax.ShapeDtypeStruct((slots, width), out_grad.dtype),
            jax.ShapeDtypeStruct((experts, tokens), jnp.float32),
            jax.ShapeDtypeStruct((slots, tokens), jnp.bfloat16),
        ],
        scratch_shapes=[
            pltpu.VMEM((tokens, width), out_grad.dtype),
            pltpu.VMEM((slots, width), out_grad.dtype),
            pltpu.VMEM((experts, tokens), jnp.float32),
            pltpu.VMEM((slots, tokens), jnp.bfloat16),
            pltpu.SemaphoreType.DMA((2,)),
            pltpu.SemaphoreType.DMA((width // cut(width, 512),)),
            pltpu.SemaphoreType.DMA((2,)),
        ],
        compiler_params=pltpu.CompilerParams(vmem_limit_bytes=56 * MIB),
        cost_estimate=pl.CostEstimate(
            flops=2 * slots * tokens * width,
            bytes_accessed=2 * (slots + tokens) * width,
            transcendentals=0,
        ),
        name="route_rows",
    )(ids_t, out_grad)


def rest_kernel(pick_ref, grad_ref, rows_hbm, rows, sem):
    spread_columns(pick_ref, lambda n, step: None, grad_ref, rows, rows_hbm, sem)


def route_rest(pick, out_grad):
    slots, tokens = pick.shape
    width = out_grad.shape[1]
    return pl.pallas_call(
        rest_kernel,
        grid=(1,),
        in_specs=[
            pl.BlockSpec((slots, tokens), lambda i: (0, 0)),
            pl.BlockSpec((tokens, width), lambda i: (0, 0)),
        ],
        out_specs=pl.BlockSpec(memory_space=pl.ANY),
        out_shape=jax.ShapeDtypeStruct((slots, width), out_grad.dtype),
        scratch_shapes=[
            pltpu.VMEM((slots, width), out_grad.dtype),
            pltpu.SemaphoreType.DMA((width // cut(width, 512),)),
        ],
        compiler_params=pltpu.CompilerParams(vmem_limit_bytes=56 * MIB),
        cost_estimate=pl.CostEstimate(
            flops=2 * slots * tokens * width,
            bytes_accessed=2 * (slots + tokens) * width,
            transcendentals=0,
        ),
        name="route_rest",
    )(pick, out_grad)


def project_kernel(start, rows_ref, weight_ref, *refs):
    if start:
        half_hbm, out_ref, total, half, sem = refs
        load = pltpu.make_async_copy(half_hbm, half, sem)
    else:
        out_ref, total = refs

    @pl.when(pl.program_id(0) == 0)
    def _():
        if start:
            load.start()
        total[...] = lax.dot_general(
            rows_ref[...], weight_ref[...], NT, preferred_element_type=jnp.float32
        )

    @pl.when(pl.program_id(0) > 0)
    def _():
        total[...] += lax.dot_general(
            rows_ref[...], weight_ref[...], NT, preferred_element_type=jnp.float32
        )

    @pl.when(pl.program_id(0) == pl.num_programs(0) - 1)
    def _():
        if start:
            load.wait()
            out_ref[...] = (total[...] + half[...]).astype(out_ref.dtype)
        else:
            out_ref[...] = total[...].astype(out_ref.dtype)


def project(rows, weight, first, half, dtype, name):
    slots, width = rows.shape
    units = weight.shape[0]
    step = cut(math.gcd(width, first) if first else width, 1024)
    start = [] if half is None else [half]
    total = pltpu.VMEM((slots, units), jnp.float32)
    return pl.pallas_call(
        functools.partial(project_kernel, half is not None),
        grid=(width // step,),
        in_specs=[
            pl.BlockSpec((slots, step), lambda i: (0, i)),
            pl.BlockSpec((units, step), lambda i: (0, i + first // step)),
        ]
        + [pl.BlockSpec(memory_space=pl.ANY)] * len(start),
        out_specs=pl.BlockSpec((slots, units), lambda i: (0, 0)),
        out_shape=jax.ShapeDtypeStruct((slots, units), dtype),
        scratch_shapes=[total] + [total, pltpu.SemaphoreType.DMA(())] * len(start),
        compiler_params=pltpu.CompilerParams(vmem_limit_bytes=56 * MIB),
        cost_estimate=pl.CostEstimate(
            flops=2 * slots * units * width,
            bytes_accessed=2 * (slots + units) * width + 4 * slots * units,
            transcendentals=0,
        ),
        name=name,
    )(rows, weight, *start)


def score_kernel(
    capacity, rows_hbm, expert_hbm, partial_ref, gates_ref, back_ref, rows, expert, score, sem
):
    slots, width = rows.shape
    bm = cut(slots, 128)
    loads = []
    for i in range(slots // bm):
        at = pl.ds(i * bm, bm)
        loads.append(
            [
                pltpu.make_async_copy(rows_hbm.at[at], rows.at[at], sem.at[0, i]),
                pltpu.make_async_copy(expert_hbm.at[at], expert.at[at], sem.at[1, i]),
            ]
        )
    ahead = 8
    for copies in loads[:ahead]:
        for copy in copies:
            copy.start()
    row = lax.broadcasted_iota(jnp.int32, (bm, 128), 0) % capacity
    lane = lax.broadcasted_iota(jnp.int32, (bm, 128), 1)
    for i, copies in enumerate(loads):
        for copy in copies:
            copy.wait()
        for copy in loads[i + ahead] if i + ahead < len(loads) else []:
            copy.start()
        at = slice(i * bm, (i + 1) * bm)
        total = partial_ref[at, :]
        for k in range(0, width, 128):
            total = total + rows[at, k : k + 128].astype(jnp.float32) * expert[
                at, k : k + 128
            ].astype(jnp.float32)
        total = jnp.sum(total, axis=1, keepdims=True)
        laid = jnp.where(row == lane, total, 0.0)
        score[i * bm // capacity : (i + 1) * bm // capacity, :] = jnp.sum(
            laid.reshape(bm // capacity, capacity, 128), axis=1
        )
    own = score[...]
    devices = own.shape[0]
    even = lax.broadcasted_iota(jnp.int32, own.shape, 0) % 2 == 0
    partner = jnp.where(even, pltpu.roll(own, devices - 1, 0), pltpu.roll(own, 1, 0))
    back_ref[...] = own + pltpu.roll(partner, capacity, 1) + gates_ref[...]


def partial_kernel(rows_ref, expert_ref, partial_ref):
    total = jnp.zeros(partial_ref.shape, jnp.float32)
    for k in range(0, rows_ref.shape[1], 128):
        total = total + rows_ref[:, k : k + 128].astype(jnp.float32) * expert_ref[
            :, k : k + 128
        ].astype(jnp.float32)
    partial_ref[...] = total


def partial_scores(rows, expert):
    slots, width = rows.shape
    bm = cut(slots, 128)
    return pl.pallas_call(
        partial_kernel,
        grid=(slots // bm,),
        in_specs=[pl.BlockSpec((bm, width), lambda i: (i, 0))] * 2,
        out_specs=pl.BlockSpec((bm, 128), lambda i: (i, 0)),
        out_shape=jax.ShapeDtypeStruct((slots, 128), jnp.float32),
        compiler_params=pltpu.CompilerParams(vmem_limit_bytes=24 * MIB),
        cost_estimate=pl.CostEstimate(
            flops=2 * slots * width, bytes_accessed=4 * slots * width, transcendentals=0
        ),
        name="partial_scores",
    )(rows, expert)


def scores(rows, expert, partial, gates, capacity):
    slots, width = rows.shape
    bm = cut(slots, 128)
    anywhere = pl.BlockSpec(memory_space=pl.ANY)
    inside = pl.BlockSpec(memory_space=pltpu.VMEM)
    return pl.pallas_call(
        functools.partial(score_kernel, capacity),
        in_specs=[anywhere, anywhere, inside, inside],
        out_specs=inside,
        out_shape=jax.ShapeDtypeStruct((slots // capacity, 128), jnp.float32),
        scratch_shapes=[
            pltpu.VMEM((slots, width), jnp.bfloat16),
            pltpu.VMEM((slots, width), jnp.bfloat16),
            pltpu.VMEM((slots // capacity, 128), jnp.float32),
            pltpu.SemaphoreType.DMA((2, slots // bm)),
        ],
        compiler_params=pltpu.CompilerParams(vmem_limit_bytes=56 * MIB),
        cost_estimate=pl.CostEstimate(
            flops=2 * slots * width, bytes_accessed=4 * slots * width, transcendentals=0
        ),
        name="score_rows",
    )(rows, expert, partial, gates)


def tiles(split, width):
    at = []
    n = 0
    while n < width:
        step = 512 if n == 0 or width - n <= 1024 else 1024
        step = min(step, (split if n < split else width) - n)
        at.append((n, step))
        n += step
    return at


def down_kernel(
    capacity, back_ref, grad_ref, hidden_hbm, proj_hbm, router_hbm, first_hbm, second_hbm,
    dw_hbm, dh_hbm, dn_hbm,
    hidden, proj, router, rows, gated, dw, dh, dn, in_sem, row_sem, dw_sem, out_sem,
):
    units, slots = hidden.shape
    split, width = first_hbm.shape[1], rows.shape[1]
    at = tiles(split, width)
    load_hidden = pltpu.make_async_copy(hidden_hbm, hidden, in_sem.at[0])
    load_proj = pltpu.make_async_copy(proj_hbm, proj, in_sem.at[1])
    load_router = pltpu.make_async_copy(router_hbm, router, in_sem.at[2])
    store_dh = pltpu.make_async_copy(dh, dh_hbm, out_sem.at[0])
    store_dn = pltpu.make_async_copy(dn, dn_hbm, out_sem.at[1])
    loads, stores = [], []
    for i, (n, step) in enumerate(at):
        columns = (slice(None), pl.ds(n, step))
        if n < split:
            source = first_hbm.at[columns]
        else:
            source = second_hbm.at[:, pl.ds(n - split, step)]
        loads.append(pltpu.make_async_copy(source, rows.at[columns], row_sem.at[i]))
        stores.append(pltpu.make_async_copy(dw.at[columns], dw_hbm.at[columns], dw_sem.at[i]))
    load_hidden.start()
    loads[0].start()

    groups = slots // capacity
    slot = lax.broadcasted_iota(jnp.int32, (groups, capacity, 128), 1)
    lane = lax.broadcasted_iota(jnp.int32, (groups, capacity, 128), 2)
    own = jnp.where(lane == slot + 2 * capacity, back_ref[...][:, None, :], 0.0)
    gate = jnp.sum(own.reshape(slots, 128), axis=1, keepdims=True)
    gate_row = jnp.broadcast_to(gate, (slots, 128)).T[0:1, :]
    load_hidden.wait()
    loads[1].start()
    gated[...] = (gate_row * hidden[...].astype(jnp.float32)).astype(gated.dtype)
    for i, (n, step) in enumerate(at):
        columns = slice(n, n + step)
        loads[i].wait()
        if i + 2 < len(loads):
            loads[i + 2].start()
        if i == 0:
            load_proj.start()
            load_router.start()
        dw[:, columns] = jnp.dot(
            gated[...], rows[:, columns], preferred_element_type=jnp.float32
        ).astype(dw.dtype)
        stores[i].start()
        if i == 1:
            load_proj.wait()
            dh[...] = (gate * proj[...].astype(jnp.float32)).astype(dh.dtype)
            store_dh.start()
            load_router.wait()
            grad = grad_ref[...].astype(jnp.float32).T.astype(jnp.bfloat16)
            dn[...] = lax.dot_general(
                grad, router[...], NT, preferred_element_type=jnp.float32
            ).astype(dn.dtype)
            store_dn.start()
    for store in stores:
        store.wait()
    store_dh.wait()
    store_dn.wait()


def down_grads(back, grad, hidden, proj, router, first, second, capacity):
    units, slots = hidden.shape
    split = first.shape[1]
    width = split + second.shape[1]
    experts, tokens = grad.shape
    count = len(tiles(split, width))
    anywhere = pl.BlockSpec(memory_space=pl.ANY)
    inside = pl.BlockSpec(memory_space=pltpu.VMEM)
    return pl.pallas_call(
        functools.partial(down_kernel, capacity),
        in_specs=[inside] * 2 + [anywhere] * 5,
        out_specs=[anywhere] * 3,
        out_shape=[
            jax.ShapeDtypeStruct((units, width), jnp.bfloat16),
            jax.ShapeDtypeStruct((slots, units), jnp.bfloat16),
            jax.ShapeDtypeStruct((tokens, width), jnp.bfloat16),
        ],
        scratch_shapes=[
            pltpu.VMEM((units, slots), jnp.bfloat16),
            pltpu.VMEM((slots, units), jnp.bfloat16),
            pltpu.VMEM((width, experts), jnp.bfloat16),
            pltpu.VMEM((slots, width), jnp.bfloat16),
            pltpu.VMEM((units, slots), jnp.bfloat16),
            pltpu.VMEM((units, width), jnp.bfloat16),
            pltpu.VMEM((slots, units), jnp.bfloat16),
            pltpu.VMEM((tokens, width), jnp.bfloat16),
            pltpu.SemaphoreType.DMA((3,)),
            pltpu.SemaphoreType.DMA((count,)),
            pltpu.SemaphoreType.DMA((count,)),
            pltpu.SemaphoreType.DMA((2,)),
        ],
        compiler_params=pltpu.CompilerParams(vmem_limit_bytes=56 * MIB),
        cost_estimate=pl.CostEstimate(
            flops=2 * slots * units * width + 2 * tokens * experts * width,
            bytes_accessed=2 * (slots + units + 2 * tokens) * width + 6 * slots * units,
            transcendentals=0,
        ),
        name="down_grads",
    )(back, grad, hidden, proj, router, first, second)


def router_kernel(
    capacity, back_ref, code_ref, prob_ref, other_code_ref, other_prob_ref, keep_ref, taken_ref,
    terms_ref, grad_ref,
):
    terms = None
    sides = ((code_ref, prob_ref, keep_ref), (other_code_ref, other_prob_ref, taken_ref))
    for side, (code, prob, normed) in enumerate(sides):
        code = code[...]
        prob = prob[...]
        gate_grad = jnp.zeros(code.shape, jnp.float32)
        for r in range(capacity):
            at = side * capacity + r
            gate_grad = jnp.where(code == r, back_ref[:, at : at + 1], gate_grad)
        prob_grad = route_scale * gate_grad
        mean = jnp.sum(prob * prob_grad, axis=0, keepdims=True)
        grad = (prob * (prob_grad - mean)).astype(jnp.bfloat16)
        if side == 0:
            grad_ref[...] = grad
        part = lax.dot_general(normed[...], grad, NT, preferred_element_type=jnp.float32)
        terms = part if side == 0 else terms + part
    terms_ref[...] = terms.astype(terms_ref.dtype)


def router_terms(back, own, other, keep, taken, capacity):
    experts = back.shape[0]
    columns, tokens = keep.shape
    return pl.pallas_call(
        functools.partial(router_kernel, capacity),
        out_shape=[
            jax.ShapeDtypeStruct((columns, experts), jnp.bfloat16),
            jax.ShapeDtypeStruct((experts, tokens), jnp.bfloat16),
        ],
        compiler_params=pltpu.CompilerParams(vmem_limit_bytes=32 * MIB),
        cost_estimate=pl.CostEstimate(
            flops=4 * columns * experts * tokens,
            bytes_accessed=4 * columns * (experts + tokens),
            transcendentals=0,
        ),
        name="router_terms",
    )(back, own[0], own[1], other[0], other[1], keep, taken)


def all_to_all(x, axes):
    return lax.all_to_all(x, axes, split_axis=0, concat_axis=0, tiled=True)


def body(out_grad, normed, router, expert_ids, hidden_act, down_weight):
    groups = lax.axis_size(ALL)
    core = lax.axis_index("c")
    tokens, width = out_grad.shape
    experts = router.shape[1]
    hidden = hidden_act[0]
    weight = down_weight[0]
    capacity = hidden.shape[0] // groups
    slots = groups * capacity
    swap = [(0, 1), (1, 0)]

    part = width * 3 // 5
    rest = width - part
    send, code_t, pick = route(expert_ids.T, out_grad, experts, capacity, part)
    first = all_to_all(send.reshape(experts, capacity, part), ALL).reshape(slots, part)
    send = route_rest(pick, out_grad[:, part:])
    expert_out = [
        jnp.dot(hidden, w, preferred_element_type=jnp.float32).astype(jnp.bfloat16)
        for w in (weight[:, :part], weight[:, part:])
    ]
    send, expert_out, hidden_t = lax.optimization_barrier((send, expert_out, hidden.T))
    second = all_to_all(send.reshape(experts, capacity, rest), ALL).reshape(slots, rest)

    logits = jnp.dot(normed, router, preferred_element_type=jnp.float32)
    prob = jax.nn.softmax(logits, axis=-1)
    gates = (route_scale * prob).astype(jnp.bfloat16)
    code = code_t.T
    slot = jnp.arange(capacity, dtype=jnp.int32).astype(jnp.float32)
    slot_gate = jnp.sum(
        jnp.where(code[None] == slot[:, None, None], gates[None].astype(jnp.float32), 0.0), axis=1
    ).astype(jnp.bfloat16)
    lanes = ((0, 0), (2 * capacity, 128 - 3 * capacity))
    gate_lanes = jnp.pad(slot_gate.astype(jnp.float32).T, lanes)

    own = (code_t, prob.T)
    other = [lax.ppermute(x, "c", swap) for x in own]
    halves = normed.T.reshape(groups // 2, 2, width // groups, tokens)
    keep = lax.dynamic_index_in_dim(halves, core, 1, keepdims=False)
    give = lax.dynamic_index_in_dim(halves, 1 - core, 1, keepdims=False)
    taken = lax.ppermute(give, "c", swap).reshape(width // 2, tokens)
    keep = keep.reshape(width // 2, tokens)

    partial = partial_scores(first, expert_out[0])
    half = project(first, weight, 0, None, jnp.float32, "project_first")
    partial, half = lax.optimization_barrier((partial, half))

    score = scores(second, expert_out[1], partial, gate_lanes, capacity)
    back = all_to_all(score, ALL)
    proj = project(second, weight, part, half, jnp.bfloat16, "project_second")

    terms, logit_grad_t = router_terms(back, own, other, keep, taken, capacity)
    got = all_to_all(terms.reshape(groups // 2, width // groups, experts), CHIPS)
    d_down, d_hidden, d_normed = down_grads(
        back, logit_grad_t, hidden_t, proj, router, first, second, capacity
    )
    d_router = jnp.sum(got.astype(jnp.float32), axis=0)
    return d_down[None], d_hidden[None], d_router, d_normed


def solution(mesh):
    dp, tensor = mesh.devices.shape
    fine = Mesh(mesh.devices.reshape(dp, tensor // 2, 2), ALL)
    in_specs = (
        P(ALL, None),
        P(ALL, None),
        P(),
        P(ALL, None),
        P(ALL, None, None),
        P(ALL, None, None),
    )
    out_specs = (P(ALL, None, None), P(ALL, None, None), P(ALL, None), P(ALL, None))
    return jax.shard_map(body, mesh=fine, in_specs=in_specs, out_specs=out_specs, check_vma=False)
```

```python
import functools
import math

import jax
import jax.numpy as jnp
from jax import lax
from jax.experimental import pallas as pl
from jax.experimental.pallas import tpu as pltpu
from jax.sharding import Mesh, PartitionSpec as P

route_scale = 16.0
ALL = ("dp", "z", "c")
CHIPS = ("dp", "z")
MIB = 1 << 20
NT = (((1,), (1,)), ((), ()))


def cut(size, best):
    return best if size % best == 0 else size


def spread_columns(pick, load, grad, rows, rows_hbm, sem):
    width = rows.shape[1]
    step = cut(width, 512)
    copies = []
    for n in range(0, width, step):
        load(n, step)
        rows[:, n : n + step] = jnp.dot(
            pick[...], grad[:, n : n + step], preferred_element_type=jnp.float32
        ).astype(rows.dtype)
        columns = (slice(None), pl.ds(n, step))
        copy = pltpu.make_async_copy(rows.at[columns], rows_hbm.at[columns], sem.at[n // step])
        copy.start()
        copies.append(copy)
    for copy in copies:
        copy.wait()


def route_kernel(
    capacity, ids_ref, grad_hbm, rows_hbm, code_hbm, pick_hbm,
    grad, rows, code_ref, pick, load_sem, sem, save_sem,
):
    width = rows.shape[1]
    half = width // 2
    loads = [
        pltpu.make_async_copy(
            grad_hbm.at[:, pl.ds(n, half)], grad.at[:, pl.ds(n, half)], load_sem.at[n // half]
        )
        for n in (0, half)
    ]
    for copy in loads:
        copy.start()
    experts, tokens = code_ref.shape
    expert = lax.broadcasted_iota(jnp.int32, (experts, tokens), 0)
    hit = ids_ref[0:1, :] == expert
    for k in range(1, ids_ref.shape[0]):
        hit = hit | (ids_ref[k : k + 1, :] == expert)
    earlier = lax.broadcasted_iota(jnp.int32, (tokens, tokens), 0)
    later = lax.broadcasted_iota(jnp.int32, (tokens, tokens), 1)
    before = jnp.where(earlier < later, 1.0, 0.0).astype(jnp.bfloat16)
    chosen = jnp.where(hit, 1.0, 0.0).astype(jnp.bfloat16)
    rank = jnp.dot(chosen, before, preferred_element_type=jnp.float32)
    code = jnp.where(hit, rank, -1.0)
    code_ref[...] = code
    slot = lax.broadcasted_iota(jnp.int32, (experts, capacity, tokens), 1).astype(jnp.float32)
    one = jnp.where(code[:, None, :] == slot, 1.0, 0.0)
    pick[...] = one.reshape(experts * capacity, tokens).astype(jnp.bfloat16)
    saves = [
        pltpu.make_async_copy(code_ref, code_hbm, save_sem.at[0]),
        pltpu.make_async_copy(pick, pick_hbm, save_sem.at[1]),
    ]
    for copy in saves:
        copy.start()

    def load(n, step):
        if n == 0:
            loads[0].wait()
        if n < half <= n + step - 1 or n == half:
            loads[1].wait()

    spread_columns(pick, load, grad, rows, rows_hbm, sem)
    for copy in saves:
        copy.wait()


def route(ids_t, out_grad, experts, capacity, width):
    tokens = out_grad.shape[0]
    slots = experts * capacity
    anywhere = pl.BlockSpec(memory_space=pl.ANY)
    return pl.pallas_call(
        functools.partial(route_kernel, capacity),
        in_specs=[pl.BlockSpec(memory_space=pltpu.VMEM), anywhere],
        out_specs=[anywhere] * 3,
        out_shape=[
            jax.ShapeDtypeStruct((slots, width), out_grad.dtype),
            jax.ShapeDtypeStruct((experts, tokens), jnp.float32),
            jax.ShapeDtypeStruct((slots, tokens), jnp.bfloat16),
        ],
        scratch_shapes=[
            pltpu.VMEM((tokens, width), out_grad.dtype),
            pltpu.VMEM((slots, width), out_grad.dtype),
            pltpu.VMEM((experts, tokens), jnp.float32),
            pltpu.VMEM((slots, tokens), jnp.bfloat16),
            pltpu.SemaphoreType.DMA((2,)),
            pltpu.SemaphoreType.DMA((width // cut(width, 512),)),
            pltpu.SemaphoreType.DMA((2,)),
        ],
        compiler_params=pltpu.CompilerParams(vmem_limit_bytes=56 * MIB),
        cost_estimate=pl.CostEstimate(
            flops=2 * slots * tokens * width,
            bytes_accessed=2 * (slots + tokens) * width,
            transcendentals=0,
        ),
        name="route_rows",
    )(ids_t, out_grad)


def rest_kernel(pick_ref, grad_ref, rows_hbm, rows, sem):
    spread_columns(pick_ref, lambda n, step: None, grad_ref, rows, rows_hbm, sem)


def route_rest(pick, out_grad):
    slots, tokens = pick.shape
    width = out_grad.shape[1]
    return pl.pallas_call(
        rest_kernel,
        grid=(1,),
        in_specs=[
            pl.BlockSpec((slots, tokens), lambda i: (0, 0)),
            pl.BlockSpec((tokens, width), lambda i: (0, 0)),
        ],
        out_specs=pl.BlockSpec(memory_space=pl.ANY),
        out_shape=jax.ShapeDtypeStruct((slots, width), out_grad.dtype),
        scratch_shapes=[
            pltpu.VMEM((slots, width), out_grad.dtype),
            pltpu.SemaphoreType.DMA((width // cut(width, 512),)),
        ],
        compiler_params=pltpu.CompilerParams(vmem_limit_bytes=56 * MIB),
        cost_estimate=pl.CostEstimate(
            flops=2 * slots * tokens * width,
            bytes_accessed=2 * (slots + tokens) * width,
            transcendentals=0,
        ),
        name="route_rest",
    )(pick, out_grad)


def project_kernel(start, rows_ref, weight_ref, *refs):
    if start:
        half_hbm, out_ref, total, half, sem = refs
        load = pltpu.make_async_copy(half_hbm, half, sem)
    else:
        out_ref, total = refs

    @pl.when(pl.program_id(0) == 0)
    def _():
        if start:
            load.start()
        total[...] = lax.dot_general(
            rows_ref[...], weight_ref[...], NT, preferred_element_type=jnp.float32
        )

    @pl.when(pl.program_id(0) > 0)
    def _():
        total[...] += lax.dot_general(
            rows_ref[...], weight_ref[...], NT, preferred_element_type=jnp.float32
        )

    @pl.when(pl.program_id(0) == pl.num_programs(0) - 1)
    def _():
        if start:
            load.wait()
            out_ref[...] = (total[...] + half[...]).astype(out_ref.dtype)
        else:
            out_ref[...] = total[...].astype(out_ref.dtype)


def project(rows, weight, first, half, dtype, name):
    slots, width = rows.shape
    units = weight.shape[0]
    step = cut(math.gcd(width, first) if first else width, 1024)
    start = [] if half is None else [half]
    total = pltpu.VMEM((slots, units), jnp.float32)
    return pl.pallas_call(
        functools.partial(project_kernel, half is not None),
        grid=(width // step,),
        in_specs=[
            pl.BlockSpec((slots, step), lambda i: (0, i)),
            pl.BlockSpec((units, step), lambda i: (0, i + first // step)),
        ]
        + [pl.BlockSpec(memory_space=pl.ANY)] * len(start),
        out_specs=pl.BlockSpec((slots, units), lambda i: (0, 0)),
        out_shape=jax.ShapeDtypeStruct((slots, units), dtype),
        scratch_shapes=[total] + [total, pltpu.SemaphoreType.DMA(())] * len(start),
        compiler_params=pltpu.CompilerParams(vmem_limit_bytes=56 * MIB),
        cost_estimate=pl.CostEstimate(
            flops=2 * slots * units * width,
            bytes_accessed=2 * (slots + units) * width + 4 * slots * units,
            transcendentals=0,
        ),
        name=name,
    )(rows, weight, *start)


def score_kernel(
    capacity, rows_hbm, expert_hbm, base_ref, back_ref, rows, expert, score, sem
):
    slots, width = rows.shape
    bm = cut(slots, 128)
    loads = []
    for i in range(slots // bm):
        at = pl.ds(i * bm, bm)
        loads.append(
            [
                pltpu.make_async_copy(rows_hbm.at[at], rows.at[at], sem.at[0, i]),
                pltpu.make_async_copy(expert_hbm.at[at], expert.at[at], sem.at[1, i]),
            ]
        )
    ahead = 8
    for copies in loads[:ahead]:
        for copy in copies:
            copy.start()
    row = lax.broadcasted_iota(jnp.int32, (bm, 128), 0) % capacity
    lane = lax.broadcasted_iota(jnp.int32, (bm, 128), 1)
    for i, copies in enumerate(loads):
        for copy in copies:
            copy.wait()
        for copy in loads[i + ahead] if i + ahead < len(loads) else []:
            copy.start()
        at = slice(i * bm, (i + 1) * bm)
        total = jnp.zeros((bm, 128), jnp.float32)
        for k in range(0, width, 128):
            total = total + rows[at, k : k + 128].astype(jnp.float32) * expert[
                at, k : k + 128
            ].astype(jnp.float32)
        total = jnp.sum(total, axis=1, keepdims=True)
        laid = jnp.where(row == lane, total, 0.0)
        score[i * bm // capacity : (i + 1) * bm // capacity, :] = jnp.sum(
            laid.reshape(bm // capacity, capacity, 128), axis=1
        )
    own = score[...]
    devices = own.shape[0]
    even = lax.broadcasted_iota(jnp.int32, own.shape, 0) % 2 == 0
    partner = jnp.where(even, pltpu.roll(own, devices - 1, 0), pltpu.roll(own, 1, 0))
    back_ref[...] = own + pltpu.roll(partner, capacity, 1) + base_ref[...]


def scores(rows, expert, base, capacity, name):
    slots, width = rows.shape
    bm = cut(slots, 128)
    anywhere = pl.BlockSpec(memory_space=pl.ANY)
    inside = pl.BlockSpec(memory_space=pltpu.VMEM)
    return pl.pallas_call(
        functools.partial(score_kernel, capacity),
        in_specs=[anywhere, anywhere, inside],
        out_specs=inside,
        out_shape=jax.ShapeDtypeStruct((slots // capacity, 128), jnp.float32),
        scratch_shapes=[
            pltpu.VMEM((slots, width), jnp.bfloat16),
            pltpu.VMEM((slots, width), jnp.bfloat16),
            pltpu.VMEM((slots // capacity, 128), jnp.float32),
            pltpu.SemaphoreType.DMA((2, slots // bm)),
        ],
        compiler_params=pltpu.CompilerParams(vmem_limit_bytes=56 * MIB),
        cost_estimate=pl.CostEstimate(
            flops=2 * slots * width, bytes_accessed=4 * slots * width, transcendentals=0
        ),
        name=name,
    )(rows, expert, base)


def tiles(split, width):
    at = []
    n = 0
    while n < width:
        step = 512 if n == 0 or width - n <= 1024 else 1024
        step = min(step, (split if n < split else width) - n)
        at.append((n, step))
        n += step
    return at


def down_kernel(
    capacity, back_ref, grad_ref, hidden_hbm, proj_hbm, router_hbm, first_hbm, second_hbm,
    dw_hbm, dh_hbm, dn_hbm,
    hidden, proj, router, rows, gated, dw, dh, dn, in_sem, row_sem, dw_sem, out_sem,
):
    units, slots = hidden.shape
    split, width = first_hbm.shape[1], rows.shape[1]
    at = tiles(split, width)
    load_hidden = pltpu.make_async_copy(hidden_hbm, hidden, in_sem.at[0])
    load_proj = pltpu.make_async_copy(proj_hbm, proj, in_sem.at[1])
    load_router = pltpu.make_async_copy(router_hbm, router, in_sem.at[2])
    store_dh = pltpu.make_async_copy(dh, dh_hbm, out_sem.at[0])
    store_dn = pltpu.make_async_copy(dn, dn_hbm, out_sem.at[1])
    loads, stores = [], []
    for i, (n, step) in enumerate(at):
        columns = (slice(None), pl.ds(n, step))
        if n < split:
            source = first_hbm.at[columns]
        else:
            source = second_hbm.at[:, pl.ds(n - split, step)]
        loads.append(pltpu.make_async_copy(source, rows.at[columns], row_sem.at[i]))
        stores.append(pltpu.make_async_copy(dw.at[columns], dw_hbm.at[columns], dw_sem.at[i]))
    load_hidden.start()
    loads[0].start()

    groups = slots // capacity
    slot = lax.broadcasted_iota(jnp.int32, (groups, capacity, 128), 1)
    lane = lax.broadcasted_iota(jnp.int32, (groups, capacity, 128), 2)
    own = jnp.where(lane == slot + 2 * capacity, back_ref[...][:, None, :], 0.0)
    gate = jnp.sum(own.reshape(slots, 128), axis=1, keepdims=True)
    gate_row = jnp.broadcast_to(gate, (slots, 128)).T[0:1, :]
    load_hidden.wait()
    loads[1].start()
    gated[...] = (gate_row * hidden[...].astype(jnp.float32)).astype(gated.dtype)
    for i, (n, step) in enumerate(at):
        columns = slice(n, n + step)
        loads[i].wait()
        if i + 2 < len(loads):
            loads[i + 2].start()
        if i == 0:
            load_proj.start()
            load_router.start()
        dw[:, columns] = jnp.dot(
            gated[...], rows[:, columns], preferred_element_type=jnp.float32
        ).astype(dw.dtype)
        stores[i].start()
        if i == 1:
            load_proj.wait()
            dh[...] = (gate * proj[...].astype(jnp.float32)).astype(dh.dtype)
            store_dh.start()
            load_router.wait()
            grad = grad_ref[...].astype(jnp.float32).T.astype(jnp.bfloat16)
            dn[...] = lax.dot_general(
                grad, router[...], NT, preferred_element_type=jnp.float32
            ).astype(dn.dtype)
            store_dn.start()
    for store in stores:
        store.wait()
    store_dh.wait()
    store_dn.wait()


def down_grads(back, grad, hidden, proj, router, first, second, capacity):
    units, slots = hidden.shape
    split = first.shape[1]
    width = split + second.shape[1]
    experts, tokens = grad.shape
    count = len(tiles(split, width))
    anywhere = pl.BlockSpec(memory_space=pl.ANY)
    inside = pl.BlockSpec(memory_space=pltpu.VMEM)
    return pl.pallas_call(
        functools.partial(down_kernel, capacity),
        in_specs=[inside] * 2 + [anywhere] * 5,
        out_specs=[anywhere] * 3,
        out_shape=[
            jax.ShapeDtypeStruct((units, width), jnp.bfloat16),
            jax.ShapeDtypeStruct((slots, units), jnp.bfloat16),
            jax.ShapeDtypeStruct((tokens, width), jnp.bfloat16),
        ],
        scratch_shapes=[
            pltpu.VMEM((units, slots), jnp.bfloat16),
            pltpu.VMEM((slots, units), jnp.bfloat16),
            pltpu.VMEM((width, experts), jnp.bfloat16),
            pltpu.VMEM((slots, width), jnp.bfloat16),
            pltpu.VMEM((units, slots), jnp.bfloat16),
            pltpu.VMEM((units, width), jnp.bfloat16),
            pltpu.VMEM((slots, units), jnp.bfloat16),
            pltpu.VMEM((tokens, width), jnp.bfloat16),
            pltpu.SemaphoreType.DMA((3,)),
            pltpu.SemaphoreType.DMA((count,)),
            pltpu.SemaphoreType.DMA((count,)),
            pltpu.SemaphoreType.DMA((2,)),
        ],
        compiler_params=pltpu.CompilerParams(vmem_limit_bytes=56 * MIB),
        cost_estimate=pl.CostEstimate(
            flops=2 * slots * units * width + 2 * tokens * experts * width,
            bytes_accessed=2 * (slots + units + 2 * tokens) * width + 6 * slots * units,
            transcendentals=0,
        ),
        name="down_grads",
    )(back, grad, hidden, proj, router, first, second)


def router_kernel(
    capacity, back_ref, code_ref, prob_ref, other_code_ref, other_prob_ref, keep_ref, taken_ref,
    terms_ref, grad_ref,
):
    terms = None
    sides = ((code_ref, prob_ref, keep_ref), (other_code_ref, other_prob_ref, taken_ref))
    for side, (code, prob, normed) in enumerate(sides):
        code = code[...]
        prob = prob[...]
        gate_grad = jnp.zeros(code.shape, jnp.float32)
        for r in range(capacity):
            at = side * capacity + r
            gate_grad = jnp.where(code == r, back_ref[:, at : at + 1], gate_grad)
        prob_grad = route_scale * gate_grad
        mean = jnp.sum(prob * prob_grad, axis=0, keepdims=True)
        grad = (prob * (prob_grad - mean)).astype(jnp.bfloat16)
        if side == 0:
            grad_ref[...] = grad
        part = lax.dot_general(normed[...], grad, NT, preferred_element_type=jnp.float32)
        terms = part if side == 0 else terms + part
    terms_ref[...] = terms.astype(terms_ref.dtype)


def router_terms(back, own, other, keep, taken, capacity):
    experts = back.shape[0]
    columns, tokens = keep.shape
    return pl.pallas_call(
        functools.partial(router_kernel, capacity),
        out_shape=[
            jax.ShapeDtypeStruct((columns, experts), jnp.bfloat16),
            jax.ShapeDtypeStruct((experts, tokens), jnp.bfloat16),
        ],
        compiler_params=pltpu.CompilerParams(vmem_limit_bytes=32 * MIB),
        cost_estimate=pl.CostEstimate(
            flops=4 * columns * experts * tokens,
            bytes_accessed=4 * columns * (experts + tokens),
            transcendentals=0,
        ),
        name="router_terms",
    )(back, own[0], own[1], other[0], other[1], keep, taken)


def all_to_all(x, axes):
    return lax.all_to_all(x, axes, split_axis=0, concat_axis=0, tiled=True)


def body(out_grad, normed, router, expert_ids, hidden_act, down_weight):
    groups = lax.axis_size(ALL)
    core = lax.axis_index("c")
    tokens, width = out_grad.shape
    experts = router.shape[1]
    hidden = hidden_act[0]
    weight = down_weight[0]
    capacity = hidden.shape[0] // groups
    slots = groups * capacity
    swap = [(0, 1), (1, 0)]

    part = width * 3 // 5
    rest = width - part
    send, code_t, pick = route(expert_ids.T, out_grad, experts, capacity, part)
    first = all_to_all(send.reshape(experts, capacity, part), ALL).reshape(slots, part)
    send = route_rest(pick, out_grad[:, part:])
    expert_out = [
        jnp.dot(hidden, w, preferred_element_type=jnp.float32).astype(jnp.bfloat16)
        for w in (weight[:, :part], weight[:, part:])
    ]
    send, expert_out, hidden_t = lax.optimization_barrier((send, expert_out, hidden.T))
    second = all_to_all(send.reshape(experts, capacity, rest), ALL).reshape(slots, rest)

    logits = jnp.dot(normed, router, preferred_element_type=jnp.float32)
    prob = jax.nn.softmax(logits, axis=-1)
    gates = (route_scale * prob).astype(jnp.bfloat16)
    code = code_t.T
    slot = jnp.arange(capacity, dtype=jnp.int32).astype(jnp.float32)
    slot_gate = jnp.sum(
        jnp.where(code[None] == slot[:, None, None], gates[None].astype(jnp.float32), 0.0), axis=1
    ).astype(jnp.bfloat16)
    lanes = ((0, 0), (2 * capacity, 128 - 3 * capacity))
    gate_lanes = jnp.pad(slot_gate.astype(jnp.float32).T, lanes)

    own = (code_t, prob.T)
    other = [lax.ppermute(x, "c", swap) for x in own]
    halves = normed.T.reshape(groups // 2, 2, width // groups, tokens)
    keep = lax.dynamic_index_in_dim(halves, core, 1, keepdims=False)
    give = lax.dynamic_index_in_dim(halves, 1 - core, 1, keepdims=False)
    taken = lax.ppermute(give, "c", swap).reshape(width // 2, tokens)
    keep = keep.reshape(width // 2, tokens)

    base = scores(first, expert_out[0], gate_lanes, capacity, "score_first")
    half = project(first, weight, 0, None, jnp.float32, "project_first")
    base, half = lax.optimization_barrier((base, half))

    score = scores(second, expert_out[1], base, capacity, "score_rows")
    back = all_to_all(score, ALL)
    proj = project(second, weight, part, half, jnp.bfloat16, "project_second")

    terms, logit_grad_t = router_terms(back, own, other, keep, taken, capacity)
    got = all_to_all(terms.reshape(groups // 2, width // groups, experts), CHIPS)
    d_down, d_hidden, d_normed = down_grads(
        back, logit_grad_t, hidden_t, proj, router, first, second, capacity
    )
    d_router = jnp.sum(got.astype(jnp.float32), axis=0)
    return d_down[None], d_hidden[None], d_router, d_normed


def solution(mesh):
    dp, tensor = mesh.devices.shape
    fine = Mesh(mesh.devices.reshape(dp, tensor // 2, 2), ALL)
    in_specs = (
        P(ALL, None),
        P(ALL, None),
        P(),
        P(ALL, None),
        P(ALL, None, None),
        P(ALL, None, None),
    )
    out_specs = (P(ALL, None, None), P(ALL, None, None), P(ALL, None), P(ALL, None))
    return jax.shard_map(body, mesh=fine, in_specs=in_specs, out_specs=out_specs, check_vma=False)
```

```python
import functools
import math

import jax
import jax.numpy as jnp
from jax import lax
from jax.experimental import pallas as pl
from jax.experimental.pallas import tpu as pltpu
from jax.sharding import Mesh, PartitionSpec as P

route_scale = 16.0
ALL = ("dp", "z", "c")
CHIPS = ("dp", "z")
MIB = 1 << 20
NT = (((1,), (1,)), ((), ()))


def cut(size, best):
    return best if size % best == 0 else size


def spread_columns(pick, load, grad, rows, rows_hbm, sem):
    width = rows.shape[1]
    step = cut(width, 512)
    copies = []
    for n in range(0, width, step):
        load(n, step)
        rows[:, n : n + step] = jnp.dot(
            pick[...], grad[:, n : n + step], preferred_element_type=jnp.float32
        ).astype(rows.dtype)
        columns = (slice(None), pl.ds(n, step))
        copy = pltpu.make_async_copy(rows.at[columns], rows_hbm.at[columns], sem.at[n // step])
        copy.start()
        copies.append(copy)
    for copy in copies:
        copy.wait()


def route_kernel(
    capacity, ids_ref, grad_hbm, rows_hbm, code_hbm, pick_hbm,
    grad, rows, code_ref, pick, load_sem, sem, save_sem,
):
    width = rows.shape[1]
    half = width // 2
    loads = [
        pltpu.make_async_copy(
            grad_hbm.at[:, pl.ds(n, half)], grad.at[:, pl.ds(n, half)], load_sem.at[n // half]
        )
        for n in (0, half)
    ]
    for copy in loads:
        copy.start()
    experts, tokens = code_ref.shape
    expert = lax.broadcasted_iota(jnp.int32, (experts, tokens), 0)
    hit = ids_ref[0:1, :] == expert
    for k in range(1, ids_ref.shape[0]):
        hit = hit | (ids_ref[k : k + 1, :] == expert)
    earlier = lax.broadcasted_iota(jnp.int32, (tokens, tokens), 0)
    later = lax.broadcasted_iota(jnp.int32, (tokens, tokens), 1)
    before = jnp.where(earlier < later, 1.0, 0.0).astype(jnp.bfloat16)
    chosen = jnp.where(hit, 1.0, 0.0).astype(jnp.bfloat16)
    rank = jnp.dot(chosen, before, preferred_element_type=jnp.float32)
    code = jnp.where(hit, rank, -1.0)
    code_ref[...] = code
    slot = lax.broadcasted_iota(jnp.int32, (experts, capacity, tokens), 1).astype(jnp.float32)
    one = jnp.where(code[:, None, :] == slot, 1.0, 0.0)
    pick[...] = one.reshape(experts * capacity, tokens).astype(jnp.bfloat16)
    saves = [
        pltpu.make_async_copy(code_ref, code_hbm, save_sem.at[0]),
        pltpu.make_async_copy(pick, pick_hbm, save_sem.at[1]),
    ]
    for copy in saves:
        copy.start()

    def load(n, step):
        if n == 0:
            loads[0].wait()
        if n < half <= n + step - 1 or n == half:
            loads[1].wait()

    spread_columns(pick, load, grad, rows, rows_hbm, sem)
    for copy in saves:
        copy.wait()


def route(ids_t, out_grad, experts, capacity, width):
    tokens = out_grad.shape[0]
    slots = experts * capacity
    anywhere = pl.BlockSpec(memory_space=pl.ANY)
    return pl.pallas_call(
        functools.partial(route_kernel, capacity),
        in_specs=[pl.BlockSpec(memory_space=pltpu.VMEM), anywhere],
        out_specs=[anywhere] * 3,
        out_shape=[
            jax.ShapeDtypeStruct((slots, width), out_grad.dtype),
            jax.ShapeDtypeStruct((experts, tokens), jnp.float32),
            jax.ShapeDtypeStruct((slots, tokens), jnp.bfloat16),
        ],
        scratch_shapes=[
            pltpu.VMEM((tokens, width), out_grad.dtype),
            pltpu.VMEM((slots, width), out_grad.dtype),
            pltpu.VMEM((experts, tokens), jnp.float32),
            pltpu.VMEM((slots, tokens), jnp.bfloat16),
            pltpu.SemaphoreType.DMA((2,)),
            pltpu.SemaphoreType.DMA((width // cut(width, 512),)),
            pltpu.SemaphoreType.DMA((2,)),
        ],
        compiler_params=pltpu.CompilerParams(vmem_limit_bytes=56 * MIB),
        cost_estimate=pl.CostEstimate(
            flops=2 * slots * tokens * width,
            bytes_accessed=2 * (slots + tokens) * width,
            transcendentals=0,
        ),
        name="route_rows",
    )(ids_t, out_grad)


def rest_kernel(pick_ref, grad_ref, rows_hbm, rows, sem):
    spread_columns(pick_ref, lambda n, step: None, grad_ref, rows, rows_hbm, sem)


def route_rest(pick, out_grad):
    slots, tokens = pick.shape
    width = out_grad.shape[1]
    return pl.pallas_call(
        rest_kernel,
        grid=(1,),
        in_specs=[
            pl.BlockSpec((slots, tokens), lambda i: (0, 0)),
            pl.BlockSpec((tokens, width), lambda i: (0, 0)),
        ],
        out_specs=pl.BlockSpec(memory_space=pl.ANY),
        out_shape=jax.ShapeDtypeStruct((slots, width), out_grad.dtype),
        scratch_shapes=[
            pltpu.VMEM((slots, width), out_grad.dtype),
            pltpu.SemaphoreType.DMA((width // cut(width, 512),)),
        ],
        compiler_params=pltpu.CompilerParams(vmem_limit_bytes=56 * MIB),
        cost_estimate=pl.CostEstimate(
            flops=2 * slots * tokens * width,
            bytes_accessed=2 * (slots + tokens) * width,
            transcendentals=0,
        ),
        name="route_rest",
    )(pick, out_grad)


def project_kernel(start, rows_ref, weight_ref, *refs):
    if start:
        half_hbm, out_ref, total, half, sem = refs
        load = pltpu.make_async_copy(half_hbm, half, sem)
    else:
        out_ref, total = refs

    @pl.when(pl.program_id(0) == 0)
    def _():
        if start:
            load.start()
        total[...] = lax.dot_general(
            rows_ref[...], weight_ref[...], NT, preferred_element_type=jnp.float32
        )

    @pl.when(pl.program_id(0) > 0)
    def _():
        total[...] += lax.dot_general(
            rows_ref[...], weight_ref[...], NT, preferred_element_type=jnp.float32
        )

    @pl.when(pl.program_id(0) == pl.num_programs(0) - 1)
    def _():
        if start:
            load.wait()
            out_ref[...] = (total[...] + half[...]).astype(out_ref.dtype)
        else:
            out_ref[...] = total[...].astype(out_ref.dtype)


def project(rows, weight, first, half, dtype, name):
    slots, width = rows.shape
    units = weight.shape[0]
    step = cut(math.gcd(width, first) if first else width, 1024)
    start = [] if half is None else [half]
    total = pltpu.VMEM((slots, units), jnp.float32)
    return pl.pallas_call(
        functools.partial(project_kernel, half is not None),
        grid=(width // step,),
        in_specs=[
            pl.BlockSpec((slots, step), lambda i: (0, i)),
            pl.BlockSpec((units, step), lambda i: (0, i + first // step)),
        ]
        + [pl.BlockSpec(memory_space=pl.ANY)] * len(start),
        out_specs=pl.BlockSpec((slots, units), lambda i: (0, 0)),
        out_shape=jax.ShapeDtypeStruct((slots, units), dtype),
        scratch_shapes=[total] + [total, pltpu.SemaphoreType.DMA(())] * len(start),
        compiler_params=pltpu.CompilerParams(vmem_limit_bytes=56 * MIB),
        cost_estimate=pl.CostEstimate(
            flops=2 * slots * units * width,
            bytes_accessed=2 * (slots + units) * width + 4 * slots * units,
            transcendentals=0,
        ),
        name=name,
    )(rows, weight, *start)


def score_kernel(
    capacity, rows_hbm, expert_hbm, base_ref, back_ref, rows, expert, score, sem
):
    slots, width = rows.shape
    bm = cut(slots, 128)
    loads = []
    for i in range(slots // bm):
        at = pl.ds(i * bm, bm)
        loads.append(
            [
                pltpu.make_async_copy(rows_hbm.at[at], rows.at[at], sem.at[0, i]),
                pltpu.make_async_copy(expert_hbm.at[at], expert.at[at], sem.at[1, i]),
            ]
        )
    ahead = 8
    for copies in loads[:ahead]:
        for copy in copies:
            copy.start()
    row = lax.broadcasted_iota(jnp.int32, (bm, 128), 0) % capacity
    lane = lax.broadcasted_iota(jnp.int32, (bm, 128), 1)
    for i, copies in enumerate(loads):
        for copy in copies:
            copy.wait()
        for copy in loads[i + ahead] if i + ahead < len(loads) else []:
            copy.start()
        at = slice(i * bm, (i + 1) * bm)
        total = jnp.zeros((bm, 128), jnp.float32)
        for k in range(0, width, 128):
            total = total + rows[at, k : k + 128].astype(jnp.float32) * expert[
                at, k : k + 128
            ].astype(jnp.float32)
        total = jnp.sum(total, axis=1, keepdims=True)
        laid = jnp.where(row == lane, total, 0.0)
        score[i * bm // capacity : (i + 1) * bm // capacity, :] = jnp.sum(
            laid.reshape(bm // capacity, capacity, 128), axis=1
        )
    own = score[...]
    devices = own.shape[0]
    even = lax.broadcasted_iota(jnp.int32, own.shape, 0) % 2 == 0
    partner = jnp.where(even, pltpu.roll(own, devices - 1, 0), pltpu.roll(own, 1, 0))
    back_ref[...] = own + pltpu.roll(partner, capacity, 1) + base_ref[...]


def scores(rows, expert, base, capacity, name):
    slots, width = rows.shape
    bm = cut(slots, 128)
    anywhere = pl.BlockSpec(memory_space=pl.ANY)
    inside = pl.BlockSpec(memory_space=pltpu.VMEM)
    return pl.pallas_call(
        functools.partial(score_kernel, capacity),
        in_specs=[anywhere, anywhere, inside],
        out_specs=inside,
        out_shape=jax.ShapeDtypeStruct((slots // capacity, 128), jnp.float32),
        scratch_shapes=[
            pltpu.VMEM((slots, width), jnp.bfloat16),
            pltpu.VMEM((slots, width), jnp.bfloat16),
            pltpu.VMEM((slots // capacity, 128), jnp.float32),
            pltpu.SemaphoreType.DMA((2, slots // bm)),
        ],
        compiler_params=pltpu.CompilerParams(vmem_limit_bytes=56 * MIB),
        cost_estimate=pl.CostEstimate(
            flops=2 * slots * width, bytes_accessed=4 * slots * width, transcendentals=0
        ),
        name=name,
    )(rows, expert, base)


def tiles(split, width):
    at = []
    n = 0
    while n < width:
        step = 512 if n == 0 or width - n <= 1024 else 1024
        step = min(step, (split if n < split else width) - n)
        at.append((n, step))
        n += step
    return at


def down_kernel(
    capacity, back_ref, grad_ref, hidden_hbm, proj_hbm, router_hbm, first_hbm, second_hbm,
    dw_hbm, dh_hbm, dn_hbm,
    hidden, proj, router, rows, gated, dw, dh, dn, in_sem, row_sem, dw_sem, out_sem,
):
    units, slots = hidden.shape
    split, width = first_hbm.shape[1], rows.shape[1]
    at = tiles(split, width)
    load_hidden = pltpu.make_async_copy(hidden_hbm, hidden, in_sem.at[0])
    load_proj = pltpu.make_async_copy(proj_hbm, proj, in_sem.at[1])
    load_router = pltpu.make_async_copy(router_hbm, router, in_sem.at[2])
    store_dh = pltpu.make_async_copy(dh, dh_hbm, out_sem.at[0])
    store_dn = pltpu.make_async_copy(dn, dn_hbm, out_sem.at[1])
    loads, stores = [], []
    for i, (n, step) in enumerate(at):
        columns = (slice(None), pl.ds(n, step))
        if n < split:
            source = first_hbm.at[columns]
        else:
            source = second_hbm.at[:, pl.ds(n - split, step)]
        loads.append(pltpu.make_async_copy(source, rows.at[columns], row_sem.at[i]))
        stores.append(pltpu.make_async_copy(dw.at[columns], dw_hbm.at[columns], dw_sem.at[i]))
    load_hidden.start()
    loads[0].start()

    groups = slots // capacity
    slot = lax.broadcasted_iota(jnp.int32, (groups, capacity, 128), 1)
    lane = lax.broadcasted_iota(jnp.int32, (groups, capacity, 128), 2)
    own = jnp.where(lane == slot + 2 * capacity, back_ref[...][:, None, :], 0.0)
    gate = jnp.sum(own.reshape(slots, 128), axis=1, keepdims=True)
    gate_row = jnp.broadcast_to(gate, (slots, 128)).T[0:1, :]
    load_hidden.wait()
    loads[1].start()
    gated[...] = gate_row.astype(gated.dtype) * hidden[...]
    for i, (n, step) in enumerate(at):
        columns = slice(n, n + step)
        loads[i].wait()
        if i + 2 < len(loads):
            loads[i + 2].start()
        if i == 0:
            load_proj.start()
            load_router.start()
        dw[:, columns] = jnp.dot(
            gated[...], rows[:, columns], preferred_element_type=jnp.float32
        ).astype(dw.dtype)
        stores[i].start()
        if i == 1:
            load_proj.wait()
            dh[...] = gate.astype(dh.dtype) * proj[...]
            store_dh.start()
            load_router.wait()
            grad = grad_ref[...].astype(jnp.float32).T.astype(jnp.bfloat16)
            dn[...] = lax.dot_general(
                grad, router[...], NT, preferred_element_type=jnp.float32
            ).astype(dn.dtype)
            store_dn.start()
    for store in stores:
        store.wait()
    store_dh.wait()
    store_dn.wait()


def down_grads(back, grad, hidden, proj, router, first, second, capacity):
    units, slots = hidden.shape
    split = first.shape[1]
    width = split + second.shape[1]
    experts, tokens = grad.shape
    count = len(tiles(split, width))
    anywhere = pl.BlockSpec(memory_space=pl.ANY)
    inside = pl.BlockSpec(memory_space=pltpu.VMEM)
    return pl.pallas_call(
        functools.partial(down_kernel, capacity),
        in_specs=[inside] * 2 + [anywhere] * 5,
        out_specs=[anywhere] * 3,
        out_shape=[
            jax.ShapeDtypeStruct((units, width), jnp.bfloat16),
            jax.ShapeDtypeStruct((slots, units), jnp.bfloat16),
            jax.ShapeDtypeStruct((tokens, width), jnp.bfloat16),
        ],
        scratch_shapes=[
            pltpu.VMEM((units, slots), jnp.bfloat16),
            pltpu.VMEM((slots, units), jnp.bfloat16),
            pltpu.VMEM((width, experts), jnp.bfloat16),
            pltpu.VMEM((slots, width), jnp.bfloat16),
            pltpu.VMEM((units, slots), jnp.bfloat16),
            pltpu.VMEM((units, width), jnp.bfloat16),
            pltpu.VMEM((slots, units), jnp.bfloat16),
            pltpu.VMEM((tokens, width), jnp.bfloat16),
            pltpu.SemaphoreType.DMA((3,)),
            pltpu.SemaphoreType.DMA((count,)),
            pltpu.SemaphoreType.DMA((count,)),
            pltpu.SemaphoreType.DMA((2,)),
        ],
        compiler_params=pltpu.CompilerParams(vmem_limit_bytes=56 * MIB),
        cost_estimate=pl.CostEstimate(
            flops=2 * slots * units * width + 2 * tokens * experts * width,
            bytes_accessed=2 * (slots + units + 2 * tokens) * width + 6 * slots * units,
            transcendentals=0,
        ),
        name="down_grads",
    )(back, grad, hidden, proj, router, first, second)


def router_kernel(
    capacity, back_ref, code_ref, prob_ref, other_code_ref, other_prob_ref, keep_ref, taken_ref,
    terms_ref, grad_ref,
):
    terms = None
    sides = ((code_ref, prob_ref, keep_ref), (other_code_ref, other_prob_ref, taken_ref))
    for side, (code, prob, normed) in enumerate(sides):
        code = code[...]
        prob = prob[...]
        gate_grad = jnp.zeros(code.shape, jnp.float32)
        for r in range(capacity):
            at = side * capacity + r
            gate_grad = jnp.where(code == r, back_ref[:, at : at + 1], gate_grad)
        prob_grad = route_scale * gate_grad
        mean = jnp.sum(prob * prob_grad, axis=0, keepdims=True)
        grad = (prob * (prob_grad - mean)).astype(jnp.bfloat16)
        if side == 0:
            grad_ref[...] = grad
        part = lax.dot_general(normed[...], grad, NT, preferred_element_type=jnp.float32)
        terms = part if side == 0 else terms + part
    terms_ref[...] = terms.astype(terms_ref.dtype)


def router_terms(back, own, other, keep, taken, capacity):
    experts = back.shape[0]
    columns, tokens = keep.shape
    return pl.pallas_call(
        functools.partial(router_kernel, capacity),
        out_shape=[
            jax.ShapeDtypeStruct((columns, experts), jnp.bfloat16),
            jax.ShapeDtypeStruct((experts, tokens), jnp.bfloat16),
        ],
        compiler_params=pltpu.CompilerParams(vmem_limit_bytes=32 * MIB),
        cost_estimate=pl.CostEstimate(
            flops=4 * columns * experts * tokens,
            bytes_accessed=4 * columns * (experts + tokens),
            transcendentals=0,
        ),
        name="router_terms",
    )(back, own[0], own[1], other[0], other[1], keep, taken)


def all_to_all(x, axes):
    return lax.all_to_all(x, axes, split_axis=0, concat_axis=0, tiled=True)


def body(out_grad, normed, router, expert_ids, hidden_act, down_weight):
    groups = lax.axis_size(ALL)
    core = lax.axis_index("c")
    tokens, width = out_grad.shape
    experts = router.shape[1]
    hidden = hidden_act[0]
    weight = down_weight[0]
    capacity = hidden.shape[0] // groups
    slots = groups * capacity
    swap = [(0, 1), (1, 0)]

    part = width * 3 // 5
    rest = width - part
    send, code_t, pick = route(expert_ids.T, out_grad, experts, capacity, part)
    first = all_to_all(send.reshape(experts, capacity, part), ALL).reshape(slots, part)
    send = route_rest(pick, out_grad[:, part:])
    expert_out = [
        jnp.dot(hidden, w, preferred_element_type=jnp.float32).astype(jnp.bfloat16)
        for w in (weight[:, :part], weight[:, part:])
    ]
    send, expert_out, hidden_t = lax.optimization_barrier((send, expert_out, hidden.T))
    second = all_to_all(send.reshape(experts, capacity, rest), ALL).reshape(slots, rest)

    logits = jnp.dot(normed, router, preferred_element_type=jnp.float32)
    prob = jax.nn.softmax(logits, axis=-1)
    gates = (route_scale * prob).astype(jnp.bfloat16)
    code = code_t.T
    slot = jnp.arange(capacity, dtype=jnp.int32).astype(jnp.float32)
    slot_gate = jnp.sum(
        jnp.where(code[None] == slot[:, None, None], gates[None].astype(jnp.float32), 0.0), axis=1
    ).astype(jnp.bfloat16)
    lanes = ((0, 0), (2 * capacity, 128 - 3 * capacity))
    gate_lanes = jnp.pad(slot_gate.astype(jnp.float32).T, lanes)

    own = (code_t, prob.T)
    other = [lax.ppermute(x, "c", swap) for x in own]
    halves = normed.T.reshape(groups // 2, 2, width // groups, tokens)
    keep = lax.dynamic_index_in_dim(halves, core, 1, keepdims=False)
    give = lax.dynamic_index_in_dim(halves, 1 - core, 1, keepdims=False)
    taken = lax.ppermute(give, "c", swap).reshape(width // 2, tokens)
    keep = keep.reshape(width // 2, tokens)

    base = scores(first, expert_out[0], gate_lanes, capacity, "score_first")
    half = project(first, weight, 0, None, jnp.float32, "project_first")
    base, half = lax.optimization_barrier((base, half))

    score = scores(second, expert_out[1], base, capacity, "score_rows")
    back = all_to_all(score, ALL)
    proj = project(second, weight, part, half, jnp.bfloat16, "project_second")

    terms, logit_grad_t = router_terms(back, own, other, keep, taken, capacity)
    got = all_to_all(terms.reshape(groups // 2, width // groups, experts), CHIPS)
    d_down, d_hidden, d_normed = down_grads(
        back, logit_grad_t, hidden_t, proj, router, first, second, capacity
    )
    d_router = jnp.sum(got.astype(jnp.float32), axis=0)
    return d_down[None], d_hidden[None], d_router, d_normed


def solution(mesh):
    dp, tensor = mesh.devices.shape
    fine = Mesh(mesh.devices.reshape(dp, tensor // 2, 2), ALL)
    in_specs = (
        P(ALL, None),
        P(ALL, None),
        P(),
        P(ALL, None),
        P(ALL, None, None),
        P(ALL, None, None),
    )
    out_specs = (P(ALL, None, None), P(ALL, None, None), P(ALL, None), P(ALL, None))
    return jax.shard_map(body, mesh=fine, in_specs=in_specs, out_specs=out_specs, check_vma=False)
```
